32 devices in a mesh: dp: 4 (over y, x), vocab: 8 (over z, core).
Axes of the slice: x: 2, y: 2, z: 4, core: 2. Of those that a mesh axis runs over, the one named last changes fastest.
Arguments:
- hidden_t: bfloat16 [8192, 768], P(('dp', 'vocab')), may hold values from -6 to 6
- head: bfloat16 [8192, 10240], P('dp', 'vocab'), may hold values from -0.2 to 0.2
- teacher: bfloat16 [768, 10240], P('dp', 'vocab'), may hold values from -16 to 960
- labels: int32 [768], P('dp'), may hold values from 0 to 10239
- temps: float32 [4], replicated, may hold values from 1 to 4
- mix: float32 [2], replicated, may hold values from 0.3 to 1
Outputs:
- hidden_grad: float32 [8192, 768], P(('dp', 'vocab'))
- head_grad: bfloat16 [8192, 10240], P('dp', 'vocab')
The draws below stay inside these ranges and needn't reach their ends.
All inputs are finite; a program needn't handle non-finite values.
Results may differ from the reference program's by a relative error of at most 0.012.
Values may be sent and summed in bfloat16 or wider, within the bound.
No kernel may reach another device: no remote copies, remote signals or barrier semaphores. Data moves between devices by JAX's collectives and lax.ppermute only.
A program may use at most 128 MiB of HBM per device.

```python
import math
import jax
import jax.numpy as jnp
import numpy as np
from jax import lax

D = 8192
NTEMP = 4
VOCAB = 10240
TOKENS = 768


def draw_head(key, part):
    own_key = jax.random.fold_in(key, 11)
    values = jnp.clip(jax.random.normal(own_key, (D, VOCAB)) * 0.033, -0.2, 0.2)
    return values.astype(jnp.bfloat16)


def draw_hidden_t(key, part):
    own_key = jax.random.fold_in(key, 13)
    values = jnp.clip(jax.random.normal(own_key, (D, TOKENS)), -6.0, 6.0)
    return values.astype(jnp.bfloat16)


def draw_teacher(key, part):
    first_key = jax.random.fold_in(key, 0)
    values = jnp.clip(jax.random.normal(first_key, (TOKENS, VOCAB)) * 3.0, -12.0, 12.0)
    return values.astype(jnp.bfloat16)


def place_ends(result, key, low, top_value):
    longest = result.shape.index(max(result.shape))
    spots = []
    for shift in (0, 1):
        where = [jax.random.randint(jax.random.fold_in(key, axis), (), 0, length) for axis, length in enumerate(result.shape)]
        where[longest] = (where[longest] + shift) % result.shape[longest]
        spots.append(tuple(where))
    return result.at[spots[0]].set(low).at[spots[1]].set(top_value)


def cumulative_ranks(count, lean):
    loads = [(1 << 20) // math.isqrt(rank ** lean) + 1 for rank in range(1, count + 1)]
    deviation = 1 + sum(loads) // (1 << 30)
    return np.cumsum(np.array([max(1, weight // deviation) for weight in loads]))


def skewed_ids(rng, extent, number_of, skew):
    grid = cumulative_ranks(number_of, skew)
    pick = jax.random.randint(jax.random.fold_in(rng, 1), extent, 0, int(grid[number_of - 1]))
    grade = jnp.searchsorted(jnp.asarray(grid, jnp.int32), pick, side="right")
    return jax.random.permutation(jax.random.fold_in(rng, 2), number_of)[grade].astype(jnp.int32)


def setup_inputs(seed: int = 0) -> dict:
    key_list = jax.random.split(jax.random.key(seed), 7)
    return {
        "hidden_t": draw_hidden_t(jax.random.fold_in(key_list[6], 71), 0),
        "head": draw_head(jax.random.fold_in(key_list[6], 71), 0),
        "teacher": draw_teacher(jax.random.fold_in(key_list[6], 71), 0),
        "labels": place_ends(skewed_ids(key_list[3], (TOKENS,), VOCAB, 2), jax.random.fold_in(key_list[3], 3), 0, VOCAB - 1).astype(jnp.int32),
        "temps": jnp.clip(jnp.exp(jax.random.uniform(key_list[4], (NTEMP,), jnp.float32, math.log(1.0), math.log(4.0))), 1.0, 4.0),
        "mix": jnp.clip(jax.random.uniform(key_list[5], (2,), jnp.float32, 0.3, 1.0), 0.3, 1.0),
    }


def tempered(values):
    highest = jnp.max(values, axis=1, keepdims=True)
    expo = jnp.exp(values - highest)
    return expo / jnp.sum(expo, axis=1, keepdims=True)


def reference(hidden_t, head, teacher, labels, temps, mix):
    logits = lax.dot_general(hidden_t, head, (((0,), (0,)), ((), ())), preferred_element_type=jnp.float32)
    target = teacher.astype(jnp.float32)
    columns = jnp.arange(logits.shape[1], dtype=jnp.int32)
    onehot = (columns[None, :] == labels[:, None]).astype(jnp.float32)
    logit_grad = mix[0] * (tempered(logits) - onehot)
    for index in range(NTEMP):
        heat = temps[index]
        logit_grad = logit_grad + mix[1] * heat * (tempered(logits / heat) - tempered(target / heat))
    logit_grad = logit_grad.astype(jnp.bfloat16)
    hidden_grad = lax.dot_general(head, logit_grad, (((1,), (1,)), ((), ())), preferred_element_type=jnp.float32)
    head_grad = jnp.dot(hidden_t, logit_grad, preferred_element_type=jnp.float32).astype(jnp.bfloat16)
    return hidden_grad, head_grad
```

```python
import jax
import jax.numpy as jnp
from jax import lax
from jax.sharding import PartitionSpec as P

CHUNKS = 1


def swap(value, axis, mask):
    count = lax.axis_size(axis)
    return lax.ppermute(value, axis, [(k, k ^ mask) for k in range(count)])


def masks_far_first(count):
    mask = count // 2
    while mask:
        yield mask
        mask //= 2


def doubling(block, axis, order):
    have = {0: block}
    for mask in order:
        keys = sorted(have)
        other = swap(jnp.concatenate([have[k] for k in keys], axis=0), axis, mask)
        for place, k in enumerate(keys):
            have[k ^ mask] = other[place : place + 1]
    return jnp.concatenate([have[k] for k in sorted(have)], axis=0)


def halving(parts, axis, order, wire):
    keep = {k: parts[k] for k in range(parts.shape[0])}
    for mask in order:
        sent = [k for k in sorted(keep) if k & mask]
        other = swap(jnp.stack([keep[k].astype(wire) for k in sent]), axis, mask)
        keep = {
            k ^ mask: keep[k ^ mask].astype(jnp.float32) + other[place].astype(jnp.float32)
            for place, k in enumerate(sent)
        }
    return keep[0].astype(jnp.float32)


def merge_stats(peak, total, inverse, axis):
    for mask in reversed(list(masks_far_first(lax.axis_size(axis)))):
        other = swap(jnp.concatenate([peak[None], total], axis=0), axis, mask)
        highest = jnp.maximum(peak, other[0])
        total = total * jnp.exp((peak - highest)[None] * inverse[:, None]) + other[1:] * jnp.exp(
            (other[0] - highest)[None] * inverse[:, None]
        )
        peak = highest
    return peak, total


def local_stats(values, inverse):
    peak = jnp.max(values, axis=1)
    total = jnp.stack(
        [jnp.sum(jnp.exp((values - peak[:, None]) * inverse[k]), axis=1) for k in range(inverse.shape[0])]
    )
    return peak, total


def mixture(values, peak, total, inverse, weights):
    result = 0.0
    for k in range(inverse.shape[0]):
        result = result + jnp.exp((values - peak[:, None]) * inverse[k]) * (weights[k] / total[k])[:, None]
    return result


def shards(hidden_t, head, teacher, labels, temps, mix):
    count_dp, count_vocab = lax.axis_size("dp"), lax.axis_size("vocab")
    me_dp, me_vocab = lax.axis_index("dp"), lax.axis_index("vocab")
    rows = hidden_t.shape[0]
    tokens, width = teacher.shape
    part = tokens // CHUNKS

    by_owner = hidden_t.T.reshape(count_dp, CHUNKS, part, rows)
    own = jnp.stack([lax.dynamic_index_in_dim(by_owner, me_dp ^ r, 0, False) for r in range(count_dp)])
    head_by_owner = head.reshape(count_vocab, rows, width)
    head_rel = jnp.stack(
        [lax.dynamic_index_in_dim(head_by_owner, me_vocab ^ r, 0, False) for r in range(count_vocab)]
    )

    inverse = 1.0 / temps
    weights = mix[1] * temps
    target = teacher.astype(jnp.float32)
    peak, total = merge_stats(*local_stats(target, inverse), inverse, "vocab")
    columns = jnp.arange(width, dtype=jnp.int32)[None, :] + me_vocab * width
    fixed = mixture(target, peak, total, inverse, weights) + jnp.where(columns == labels[:, None], mix[0], 0.0)

    student_inverse = jnp.concatenate([jnp.ones((1,), jnp.float32), inverse])
    student_weights = jnp.concatenate([mix[:1], weights])
    vocab_far = list(masks_far_first(count_vocab))
    dp_far = list(masks_far_first(count_dp))

    hidden_parts, head_grad = [], 0.0
    for c in range(CHUNKS):
        dp_order = dp_far if c % 2 == 0 else dp_far[::-1]
        mine = own[:, c].reshape(1, count_dp * part, rows)
        gathered = doubling(mine, "vocab", vocab_far)
        logits = lax.dot_general(
            gathered, head_rel, (((0, 2), (0, 1)), ((), ())), preferred_element_type=jnp.float32
        )
        logits = halving(logits.reshape(count_dp, part, width), "dp", dp_order, jnp.float16)
        peak, total = merge_stats(*local_stats(logits, student_inverse), student_inverse, "vocab")
        grad = mixture(logits, peak, total, student_inverse, student_weights) - fixed[c * part : (c + 1) * part]
        grad_rel = doubling(grad.astype(jnp.bfloat16)[None], "dp", dp_order)
        grad_nat = jnp.concatenate(
            [lax.dynamic_index_in_dim(grad_rel, me_dp ^ r, 0, False) for r in range(count_dp)]
        )
        partial = lax.dot_general(
            head_rel, grad_nat, (((2,), (1,)), ((), ())), preferred_element_type=jnp.float32
        )
        hidden_parts.append(halving(partial, "vocab", vocab_far[::-1], jnp.bfloat16))
        gathered_nat = jnp.concatenate(
            [lax.dynamic_index_in_dim(gathered, me_vocab ^ r, 0, False) for r in range(count_vocab)], axis=1
        )
        head_grad = head_grad + lax.dot_general(
            gathered_nat,
            grad_rel.reshape(count_dp * part, width),
            (((0,), (0,)), ((), ())),
            preferred_element_type=jnp.float32,
        )
    hidden_grad = jnp.stack([p.reshape(rows, count_dp, part) for p in hidden_parts], axis=2)
    return (hidden_grad.reshape(rows, count_dp * tokens), head_grad.astype(jnp.bfloat16))


def solution(mesh):
    placed = (P(("dp", "vocab"), None), P("dp", "vocab"), P("dp", "vocab"), P("dp"), P(), P())
    return jax.shard_map(
        shards,
        mesh=mesh,
        in_specs=placed,
        out_specs=(P(("dp", "vocab"), None), P("dp", "vocab")),
        check_vma=False,
    )
```

```python
import functools

import jax
import jax.numpy as jnp
from jax import lax
from jax.experimental import pallas as pl
from jax.experimental.pallas import tpu as pltpu
from jax.sharding import PartitionSpec as P

CHUNKS = 2
STRIP = 16
LANES = 128


def swap(value, axis, mask):
    count = lax.axis_size(axis)
    return lax.ppermute(value, axis, [(k, k ^ mask) for k in range(count)])


def masks_far_first(count):
    mask = count // 2
    while mask:
        yield mask
        mask //= 2


def pick(parts, place, axis=0):
    return lax.dynamic_index_in_dim(parts, place, axis, keepdims=False)


def padded(count):
    return -(-count // LANES) * LANES


VMEM = pl.BlockSpec(memory_space=pltpu.VMEM)
SMEM = pl.BlockSpec(memory_space=pltpu.SMEM)


def stats_kernel(heats, x_ref, inverse_ref, out_ref, column):
    tokens = x_ref.shape[0]
    column[...] = jnp.zeros_like(column)
    lane = lax.broadcasted_iota(jnp.int32, (STRIP, LANES), 1)

    @pl.loop(0, tokens // STRIP)
    def _(strip):
        rows = pl.ds(pl.multiple_of(strip * STRIP, STRIP), STRIP)
        x = x_ref[rows, :].astype(jnp.float32)
        peak = jnp.max(x, axis=1, keepdims=True)
        x = x - peak
        record = jnp.where(lane == 0, peak, 0.0)
        for k in range(heats):
            total = jnp.sum(jnp.exp(x * inverse_ref[k]), axis=1, keepdims=True)
            record = jnp.where(lane == k + 1, total, record)
        column[rows, :] = record

    out_ref[...] = column[...].T[: out_ref.shape[0], :]


def local_stats(values, inverse):
    tokens, heats = values.shape[0], inverse.shape[0]
    return pl.pallas_call(
        functools.partial(stats_kernel, heats),
        out_shape=jax.ShapeDtypeStruct((8, padded(tokens)), jnp.float32),
        in_specs=[VMEM, SMEM],
        out_specs=VMEM,
        scratch_shapes=[pltpu.VMEM((padded(tokens), LANES), jnp.float32)],
        compiler_params=pltpu.CompilerParams(vmem_limit_bytes=16 << 20),
        name="stats",
    )(values, inverse)


def fixed_kernel(heats, x_ref, stats_ref, scalars_ref, out_ref, column):
    tokens, width = x_ref.shape
    column[...] = stats_ref[...].T
    lane = lax.broadcasted_iota(jnp.int32, (STRIP, width), 1).astype(jnp.float32)

    @pl.loop(0, tokens // STRIP)
    def _(strip):
        rows = pl.ds(pl.multiple_of(strip * STRIP, STRIP), STRIP)
        record = column[rows, :]
        x = x_ref[rows, :].astype(jnp.float32) - record[:, 0:1]
        result = jnp.where(lane == record[:, heats + 1 : heats + 2], scalars_ref[2 * heats], 0.0)
        for k in range(heats):
            factor = scalars_ref[heats + k] / record[:, k + 1 : k + 2]
            result = result + jnp.exp(x * scalars_ref[k]) * factor
        out_ref[rows, :] = result


def grad_kernel(heats, x_ref, stats_ref, scalars_ref, fixed_ref, out_ref, column):
    tokens = x_ref.shape[0]
    column[...] = stats_ref[...].T

    @pl.loop(0, tokens // STRIP)
    def _(strip):
        rows = pl.ds(pl.multiple_of(strip * STRIP, STRIP), STRIP)
        record = column[rows, :]
        x = x_ref[rows, :] - record[:, 0:1]
        result = -fixed_ref[rows, :]
        for k in range(heats):
            factor = scalars_ref[heats + k] / record[:, k + 1 : k + 2]
            result = result + jnp.exp(x * scalars_ref[k]) * factor
        out_ref[rows, :] = result.astype(out_ref.dtype)


def mixture(kernel, heats, values, stats, scalars, *more, dtype, name):
    return pl.pallas_call(
        functools.partial(kernel, heats),
        out_shape=jax.ShapeDtypeStruct(values.shape, dtype),
        in_specs=[VMEM, VMEM, SMEM] + [VMEM] * len(more),
        out_specs=VMEM,
        scratch_shapes=[pltpu.VMEM((padded(values.shape[0]), 8), jnp.float32)],
        compiler_params=pltpu.CompilerParams(vmem_limit_bytes=16 << 20),
        name=name,
    )(values, stats, scalars, *more)


def merge(mine, other, inverse):
    heats = inverse.shape[0]
    highest = jnp.maximum(mine[0:1], other[0:1])
    total = mine[1 : heats + 1] * jnp.exp((mine[0:1] - highest) * inverse[:, None]) + other[
        1 : heats + 1
    ] * jnp.exp((other[0:1] - highest) * inverse[:, None])
    return jnp.concatenate([highest, total, mine[heats + 1 :]], axis=0)


def send_kernel(order_ref, place_ref, head_ref, found_ref, out_ref, grad_ref):
    part = found_ref.shape[1]

    @pl.when(pl.program_id(0) == 0)
    def _():
        for n in range(found_ref.shape[0]):
            grad_ref[n * part : (n + 1) * part, :] = found_ref[place_ref[n]]

    out_ref[0] = lax.dot_general(
        head_ref[...], grad_ref[...], (((1,), (1,)), ((), ())), preferred_element_type=jnp.float32
    ).astype(out_ref.dtype)


def keep_kernel(order_ref, head_ref, grad_ref, out_ref):
    out_ref[0] = lax.dot_general(
        head_ref[...], grad_ref[...], (((1,), (1,)), ((), ())), preferred_element_type=jnp.float32
    )


def products_to_send(order, place, head, found, rows):
    blocks, width = order.shape[0], head.shape[1]
    tokens = found.shape[0] * found.shape[1]
    return pl.pallas_call(
        send_kernel,
        grid_spec=pltpu.PrefetchScalarGridSpec(
            num_scalar_prefetch=2,
            grid=(blocks,),
            in_specs=[
                pl.BlockSpec((rows, width), lambda s, order, place: (order[s], 0)),
                pl.BlockSpec(found.shape, lambda s, order, place: (0, 0, 0)),
            ],
            out_specs=[
                pl.BlockSpec((1, rows, tokens), lambda s, order, place: (s, 0, 0)),
                pl.BlockSpec((tokens, width), lambda s, order, place: (0, 0)),
            ],
        ),
        out_shape=[
            jax.ShapeDtypeStruct((blocks, rows, tokens), jnp.bfloat16),
            jax.ShapeDtypeStruct((tokens, width), jnp.bfloat16),
        ],
        compiler_params=pltpu.CompilerParams(vmem_limit_bytes=24 << 20),
        name="products_to_send",
    )(order, place, head, found)


def products_to_keep(order, head, grad, rows):
    blocks, width, tokens = order.shape[0], head.shape[1], grad.shape[0]
    return pl.pallas_call(
        keep_kernel,
        grid_spec=pltpu.PrefetchScalarGridSpec(
            num_scalar_prefetch=1,
            grid=(blocks,),
            in_specs=[
                pl.BlockSpec((rows, width), lambda s, order: (order[s], 0)),
                pl.BlockSpec((tokens, width), lambda s, order: (0, 0)),
            ],
            out_specs=pl.BlockSpec((1, rows, tokens), lambda s, order: (s, 0, 0)),
        ),
        out_shape=jax.ShapeDtypeStruct((blocks, rows, tokens), jnp.float32),
        compiler_params=pltpu.CompilerParams(vmem_limit_bytes=24 << 20),
        name="products_to_keep",
    )(order, head, grad)


def shards(hidden_t, head, teacher, labels, temps, mix):
    count_dp, count_vocab = lax.axis_size("dp"), lax.axis_size("vocab")
    me_dp, me_vocab = lax.axis_index("dp"), lax.axis_index("vocab")
    rows = hidden_t.shape[0]
    tokens, width = teacher.shape
    part = tokens // CHUNKS
    heats = temps.shape[0]
    far = list(masks_far_first(count_vocab))
    near = far[::-1]

    own = hidden_t.T.reshape(count_dp, CHUNKS, part, rows)

    inverse = 1.0 / temps
    weights = mix[1] * temps
    student_inverse = jnp.concatenate([jnp.ones((1,), jnp.float32), inverse])
    teacher_scalars = jnp.concatenate([inverse, weights, mix[:1]])
    student_scalars = jnp.concatenate([student_inverse, mix[:1], weights])
    relative = jnp.arange(0, count_vocab, 2, dtype=jnp.int32)
    keep_order = me_vocab ^ relative
    send_order = me_vocab ^ (relative + 1)
    dp_order = me_dp ^ jnp.arange(count_dp, dtype=jnp.int32)

    def gather_hidden(block):
        have = {0: block[None]}
        for mask in far:
            keys = sorted(have)
            other = swap(jnp.concatenate([have[k] for k in keys], axis=0), "vocab", mask)
            for place, k in enumerate(keys):
                have[k ^ mask] = other[place : place + 1]
        found = jnp.concatenate([have[k] for k in range(count_vocab)], axis=0)
        return jnp.concatenate([pick(found, me_vocab ^ n) for n in range(count_vocab)], axis=1)

    def partial_logits(gathered):
        partial = jnp.dot(gathered, head, preferred_element_type=jnp.float32).reshape(count_dp, part, width)
        coded = partial.astype(jnp.float16)
        return pick(partial, me_dp), [pick(coded, me_dp ^ r) for r in range(1, count_dp)]

    def merged(stats, inverse):
        for mask in near:
            stats = merge(stats, swap(stats, "vocab", mask), inverse)
        return stats

    def reduced(keep, send):
        for mask in near:
            if mask > 1:
                send = jnp.concatenate([keep[k][None] for k in range(1, keep.shape[0], 2)]).astype(jnp.bfloat16)
                keep = jnp.concatenate([keep[k][None] for k in range(0, keep.shape[0], 2)])
            keep = keep + swap(send, "vocab", mask).astype(jnp.float32)
        return keep[0]

    gathered = [gather_hidden(own[:, c].reshape(count_dp * part, rows)) for c in range(CHUNKS)]

    teacher_stats = merged(local_stats(teacher, inverse), inverse)
    place = (labels - me_vocab * width).astype(jnp.float32)
    place = jnp.pad(place, (0, teacher_stats.shape[1] - tokens))[None]
    teacher_stats = jnp.concatenate([teacher_stats[: heats + 1], place, teacher_stats[heats + 2 :]], axis=0)
    fixed = mixture(
        fixed_kernel, heats, teacher, teacher_stats, teacher_scalars, dtype=jnp.float32, name="fixed"
    )

    kept, sent, received = [], [], []
    for c in range(CHUNKS):
        if c:
            sent[c - 1][0], gathered[c] = lax.optimization_barrier((sent[c - 1][0], gathered[c]))
        mine, parts = partial_logits(gathered[c])
        kept.append(mine)
        sent.append(parts)
        received.append([swap(parts[r - 1], "dp", r) for r in range(1, count_dp)])

    grads, found = [], []
    for c in range(CHUNKS):
        if c:
            grads[c - 1], received[c] = lax.optimization_barrier((grads[c - 1], received[c]))
            found[c - 1] = [grads[c - 1]] + [swap(grads[c - 1], "dp", r) for r in range(1, count_dp)]
        logits = kept[c]
        for other in received[c]:
            logits = logits + other.astype(jnp.float32)
        stats = merged(local_stats(logits, student_inverse), student_inverse)
        grads.append(
            mixture(
                grad_kernel,
                heats + 1,
                logits,
                stats,
                student_scalars,
                fixed[c * part : (c + 1) * part],
                dtype=jnp.bfloat16,
                name="grad",
            )
        )
        found.append([grads[c]] + [swap(grads[c], "dp", r) for r in range(1, count_dp)])

    all_grads, hidden_parts = [], []
    for c in range(CHUNKS):
        if c < CHUNKS - 1:
            grads[c + 1], found[c] = lax.optimization_barrier((grads[c + 1], found[c]))
            found[c + 1] = [grads[c + 1]] + [swap(grads[c + 1], "dp", r) for r in range(1, count_dp)]
        send, grad_all = products_to_send(send_order, dp_order, head, jnp.stack(found[c]), rows)
        keep = products_to_keep(keep_order, head, grad_all, rows)
        all_grads.append(grad_all)
        hidden_parts.append(reduced(keep, send))

    head_grad = lax.dot_general(
        jnp.concatenate(gathered, axis=0),
        jnp.concatenate(all_grads, axis=0),
        (((0,), (0,)), ((), ())),
        preferred_element_type=jnp.float32,
    ).astype(jnp.bfloat16)
    hidden_grad = jnp.stack([p.reshape(rows, count_dp, part) for p in hidden_parts], axis=2)
    return (hidden_grad.reshape(rows, count_dp * tokens), head_grad)


def solution(mesh):
    placed = (P(("dp", "vocab"), None), P("dp", "vocab"), P("dp", "vocab"), P("dp"), P(), P())
    return jax.shard_map(
        shards,
        mesh=mesh,
        in_specs=placed,
        out_specs=(P(("dp", "vocab"), None), P("dp", "vocab")),
        check_vma=False,
    )
```

```python
import functools

import jax
import jax.numpy as jnp
from jax import lax
from jax.experimental import pallas as pl
from jax.experimental.pallas import tpu as pltpu
from jax.sharding import PartitionSpec as P

CHUNKS = 2
STRIP = 16
LANES = 128


def swap(value, axis, mask):
    count = lax.axis_size(axis)
    return lax.ppermute(value, axis, [(k, k ^ mask) for k in range(count)])


def masks_far_first(count):
    mask = count // 2
    while mask:
        yield mask
        mask //= 2


def pick(parts, place, axis=0):
    return lax.dynamic_index_in_dim(parts, place, axis, keepdims=False)


def padded(count):
    return -(-count // LANES) * LANES


VMEM = pl.BlockSpec(memory_space=pltpu.VMEM)
SMEM = pl.BlockSpec(memory_space=pltpu.SMEM)


def stats_kernel(heats, pieces, inverse_ref, *refs):
    *values, out_ref, column = refs
    column[...] = jnp.zeros_like(column)
    lane = lax.broadcasted_iota(jnp.int32, (STRIP, LANES), 1)
    chunks = len(values) * pieces
    part = values[0].shape[0] // pieces
    for chunk in range(chunks):
        x_ref, start = values[chunk // pieces], chunk % pieces * part
        base = chunk * padded(part)

        @pl.loop(0, part // STRIP)
        def _(strip):
            row = pl.multiple_of(strip * STRIP, STRIP)
            x = x_ref[pl.ds(start + row, STRIP), :].astype(jnp.float32)
            peak = jnp.max(x, axis=1, keepdims=True)
            x = x - peak
            record = jnp.where(lane == 0, peak, 0.0)
            for k in range(heats):
                total = jnp.sum(jnp.exp(x * inverse_ref[k]), axis=1, keepdims=True)
                record = jnp.where(lane == k + 1, total, record)
            column[pl.ds(base + row, STRIP), :] = record

    out_ref[...] = column[...].T[: out_ref.shape[0], :]


def local_stats(values, pieces, inverse):
    tokens, heats = values[0].shape[0] // pieces, inverse.shape[0]
    lanes = len(values) * pieces * padded(tokens)
    size = len(values) * values[0].size
    return pl.pallas_call(
        functools.partial(stats_kernel, heats, pieces),
        out_shape=jax.ShapeDtypeStruct((8, lanes), jnp.float32),
        in_specs=[SMEM] + [VMEM] * len(values),
        out_specs=VMEM,
        scratch_shapes=[pltpu.VMEM((lanes, LANES), jnp.float32)],
        compiler_params=pltpu.CompilerParams(vmem_limit_bytes=16 << 20),
        cost_estimate=pl.CostEstimate(flops=2 * heats * size, bytes_accessed=2 * size, transcendentals=heats * size),
        name="stats",
    )(inverse, *values)


def grad_kernel(heats, chunk, x_ref, teacher_ref, stats_ref, scalars_ref, out_ref, column):
    part, width = x_ref.shape
    column[...] = stats_ref[...].T
    lane = lax.broadcasted_iota(jnp.int32, (STRIP, width), 1).astype(jnp.float32)

    @pl.loop(0, part // STRIP)
    def _(strip):
        row = pl.multiple_of(strip * STRIP, STRIP)
        record = column[pl.ds(row, STRIP), :]
        x = x_ref[pl.ds(row, STRIP), :] - record[:, 0:1]
        t = teacher_ref[pl.ds(chunk * part + row, STRIP), :].astype(jnp.float32) - record[:, 8:9]
        result = jnp.exp(x) * (scalars_ref[1, 0] / record[:, 1:2])
        result = result - jnp.where(lane == record[:, 15:16], scalars_ref[1, 0], 0.0)
        for k in range(1, heats + 1):
            scale, factor = scalars_ref[0, k], scalars_ref[1, k]
            result = result + jnp.exp(x * scale) * (factor / record[:, k + 1 : k + 2])
            result = result - jnp.exp(t * scale) * (factor / record[:, k + 8 : k + 9])
        out_ref[pl.ds(row, STRIP), :] = result.astype(out_ref.dtype)


def logit_grad(chunk, logits, teacher, stats, scalars):
    heats = scalars.shape[1] - 1
    return pl.pallas_call(
        functools.partial(grad_kernel, heats, chunk),
        out_shape=jax.ShapeDtypeStruct(logits.shape, jnp.bfloat16),
        in_specs=[VMEM, VMEM, VMEM, SMEM],
        out_specs=VMEM,
        scratch_shapes=[pltpu.VMEM((padded(logits.shape[0]), stats.shape[0]), jnp.float32)],
        compiler_params=pltpu.CompilerParams(vmem_limit_bytes=16 << 20),
        cost_estimate=pl.CostEstimate(
            flops=6 * heats * logits.size, bytes_accessed=8 * logits.size, transcendentals=2 * heats * logits.size
        ),
        name="grad",
    )(logits, teacher, stats, scalars)


def merge(mine, other, inverse):
    heats = inverse.shape[0]
    highest = jnp.maximum(mine[0:1], other[0:1])
    total = mine[1 : heats + 1] * jnp.exp((mine[0:1] - highest) * inverse) + other[1 : heats + 1] * jnp.exp(
        (other[0:1] - highest) * inverse
    )
    return jnp.concatenate([highest, total, mine[heats + 1 :]], axis=0)


def copy_kernel(rows, order_ref, in_ref, *refs):
    *out_refs, held, come, gone = refs
    inward, outward = [], []
    for side, out_ref in enumerate(out_refs):
        for k in range(out_ref.shape[0]):
            start = pl.multiple_of(order_ref[side, k] * rows, rows)
            slot = side * out_ref.shape[0] + k
            inward.append(pltpu.make_async_copy(in_ref.at[pl.ds(start, rows)], held.at[slot], come.at[slot]))
            outward.append(pltpu.make_async_copy(held.at[slot], out_ref.at[k], gone.at[slot]))
    for copy in inward:
        copy.start()
    for come_copy, gone_copy in zip(inward, outward):
        come_copy.wait()
        gone_copy.start()
    for copy in outward:
        copy.wait()


def row_blocks(array, order, rows):
    sides, count = order.shape
    block = jax.ShapeDtypeStruct((count, rows, array.shape[1]), array.dtype)
    hbm = pl.BlockSpec(memory_space=pltpu.HBM)
    return pl.pallas_call(
        functools.partial(copy_kernel, rows),
        out_shape=[block] * sides,
        in_specs=[SMEM, hbm],
        out_specs=[hbm] * sides,
        scratch_shapes=[
            pltpu.VMEM((sides * count, rows, array.shape[1]), array.dtype),
            pltpu.SemaphoreType.DMA((sides * count,)),
            pltpu.SemaphoreType.DMA((sides * count,)),
        ],
        compiler_params=pltpu.CompilerParams(vmem_limit_bytes=16 << 20),
        cost_estimate=pl.CostEstimate(flops=0, bytes_accessed=4 * array.size, transcendentals=0),
        name="row_blocks",
    )(order, array)


def shards(hidden_t, head, teacher, labels, temps, mix):
    count_dp, count_vocab = lax.axis_size("dp"), lax.axis_size("vocab")
    me_dp, me_vocab = lax.axis_index("dp"), lax.axis_index("vocab")
    rows = hidden_t.shape[0]
    tokens, width = teacher.shape
    part = tokens // CHUNKS
    heats = temps.shape[0]
    far = list(masks_far_first(count_vocab))
    near = far[::-1]
    dp_masks = list(masks_far_first(count_dp))

    own = hidden_t.T.reshape(count_dp, CHUNKS, part, rows).transpose(1, 0, 2, 3).reshape(-1, rows)

    inverse = 1.0 / temps
    weights = mix[1] * temps
    student_inverse = jnp.concatenate([jnp.ones((1,), jnp.float32), inverse])
    scalars = jnp.stack([student_inverse, jnp.concatenate([mix[:1], weights])])
    relative = jnp.arange(0, count_vocab, 2, dtype=jnp.int32)
    keep_order = me_vocab ^ relative
    send_order = me_vocab ^ (relative + 1)

    def partial_logits(gathered):
        partial = jnp.dot(gathered, head, preferred_element_type=jnp.float32)
        return partial.reshape(*[2] * len(dp_masks), part, width)

    def reduced(partial, masks):
        left = dp_masks
        for mask in masks:
            axis, bit = left.index(mask), (me_dp // mask) % 2
            other = swap(pick(partial, 1 - bit, axis).astype(jnp.float16), "dp", mask)
            partial = pick(partial, bit, axis) + other.astype(jnp.float32)
            left = [m for m in left if m != mask]
        return partial

    def merged(student, fixed):
        stats = jnp.concatenate([student, fixed])
        for mask in near:
            other = swap(stats, "vocab", mask)
            stats = jnp.concatenate(
                [
                    merge(stats[:8], other[:8], student_inverse[:, None]),
                    merge(stats[8:], other[8:], inverse[:, None]),
                ]
            )
        return stats

    def products(blocks, grad):
        return lax.dot_general(blocks, grad, (((2,), (1,)), ((), ())), preferred_element_type=jnp.float32)

    def folded(keep, send):
        keep = keep + send.astype(jnp.float32)
        rest = [keep[k][None] for k in range(keep.shape[0])]
        if len(rest) == 1:
            return keep, None
        return jnp.concatenate(rest[0::2]), jnp.concatenate(rest[1::2]).astype(jnp.bfloat16)

    have, cross = [], []
    for c in range(CHUNKS):
        block = own[c * count_dp * part : (c + 1) * count_dp * part][None]
        have.append({0: block})
        cross.append({1: swap(block, "vocab", 1)})
    own_stats = local_stats([teacher], CHUNKS, inverse)
    for step in range(len(far) - 1):
        arrived = []
        for c in range(CHUNKS):
            mask = far[:-1][step] if c % 2 else near[1:][step]
            keys = sorted(have[c])
            arrived.append((keys, mask, swap(jnp.concatenate([have[c][k] for k in keys]), "vocab", mask)))
        for c, (keys, mask, other) in enumerate(arrived):
            other_cross = swap(other, "vocab", 1)
            for place, k in enumerate(keys):
                have[c][k ^ mask] = other[place : place + 1]
                cross[c][k ^ mask ^ 1] = other_cross[place : place + 1]
        if step == 0:
            own_stats, have = lax.optimization_barrier((own_stats, have))
            head_send, head_keep = row_blocks(head, jnp.stack([send_order, keep_order]), rows)

    (head_send, head_keep), have, cross = lax.optimization_barrier(((head_send, head_keep), have, cross))
    gathered, partials = [], []
    for c in range(CHUNKS):
        found = have[c] | cross[c]
        found = jnp.concatenate([found[k] for k in range(count_vocab)])
        gathered.append(jnp.concatenate([pick(found, me_vocab ^ n) for n in range(count_vocab)], axis=1))
        partials.append(partial_logits(gathered[c]))
    logits = [
        reduced(partials[c], dp_masks if c % 2 else dp_masks[::-1]) for c in range(CHUNKS)
    ]
    place = (labels - me_vocab * width).astype(jnp.float32).reshape(CHUNKS, part)
    place = jnp.pad(place, ((0, 0), (0, padded(part) - part))).reshape(1, -1)
    stats = merged(local_stats(logits, 1, student_inverse), own_stats)
    stats = jnp.split(jnp.concatenate([stats[:15], place]), CHUNKS, axis=1)

    grads, arrived = [], []
    for c in range(CHUNKS):
        grad = logit_grad(c, logits[c], teacher, stats[c], scalars)
        if c + 1 < CHUNKS:
            grad, logits[c + 1] = lax.optimization_barrier((grad, logits[c + 1]))
        grads.append(grad)
        arrived.append([swap(grad, "dp", r) for r in range(1, count_dp)])

    all_grads, state = [], []
    for c in range(CHUNKS):
        if c + 1 < CHUNKS:
            grads[c + 1], arrived[c] = lax.optimization_barrier((grads[c + 1], arrived[c]))
            arrived[c + 1] = [swap(grads[c + 1], "dp", r) for r in range(1, count_dp)]
        found = jnp.stack([grads[c]] + arrived[c])
        grad_all = jnp.concatenate([pick(found, me_dp ^ n) for n in range(count_dp)])
        grad_all = lax.optimization_barrier(grad_all)
        all_grads.append(grad_all)
        crossed = swap(products(head_send, grad_all).astype(jnp.bfloat16), "vocab", 1)
        if c + 1 < CHUNKS:
            pass
        else:
            state[c - 1], crossed = lax.optimization_barrier((state[c - 1], crossed))
        state.append(folded(products(head_keep, grad_all), crossed))
        if c + 1 < CHUNKS:
            keep, send = state[c]
            state[c] = folded(keep, swap(send, "vocab", near[1]))
            arrived[c + 1], state[c] = lax.optimization_barrier((arrived[c + 1], state[c]))
    (state, all_grads) = lax.optimization_barrier((state, all_grads))
    head_grad = lax.dot_general(
        jnp.concatenate(gathered, axis=0),
        jnp.concatenate(all_grads, axis=0),
        (((0,), (0,)), ((), ())),
        preferred_element_type=jnp.float32,
    ).astype(jnp.bfloat16)
    for place, mask in enumerate(near[1:]):
        for c in range(CHUNKS):
            if place == 0 and c + 1 < CHUNKS:
                continue
            keep, send = state[c]
            state[c] = folded(keep, swap(send, "vocab", mask))
    hidden_parts = [keep[0] for keep, _ in state]
    hidden_grad = jnp.stack([p.reshape(rows, count_dp, part) for p in hidden_parts], axis=2)
    return (hidden_grad.reshape(rows, count_dp * tokens), head_grad)


def solution(mesh):
    placed = (P(("dp", "vocab"), None), P("dp", "vocab"), P("dp", "vocab"), P("dp"), P(), P())
    return jax.shard_map(
        shards,
        mesh=mesh,
        in_specs=placed,
        out_specs=(P(("dp", "vocab"), None), P("dp", "vocab")),
        check_vma=False,
    )
```

```python
import functools

import jax
import jax.numpy as jnp
from jax import lax
from jax.experimental import pallas as pl
from jax.experimental.pallas import tpu as pltpu
from jax.sharding import PartitionSpec as P

CHUNKS = 2
FIRST = 64
STRIP = 32
LANES = 128
LOG2E = 1.4426950408889634


def swap(value, axis, mask):
    count = lax.axis_size(axis)
    return lax.ppermute(value, axis, [(k, k ^ mask) for k in range(count)])


def masks_far_first(count):
    mask = count // 2
    while mask:
        yield mask
        mask //= 2


def pick(parts, place, axis=0):
    return lax.dynamic_index_in_dim(parts, place, axis, keepdims=False)


def padded(count):
    return -(-count // LANES) * LANES


VMEM = pl.BlockSpec(memory_space=pltpu.VMEM)
SMEM = pl.BlockSpec(memory_space=pltpu.SMEM)


def stats_kernel(heats, pieces, inverse_ref, *refs):
    *values, out_ref, column = refs
    column[...] = jnp.zeros_like(column)
    lane = lax.broadcasted_iota(jnp.int32, (STRIP, LANES), 1)
    chunks = len(values) * pieces
    part = values[0].shape[0] // pieces
    for chunk in range(chunks):
        x_ref, start = values[chunk // pieces], chunk % pieces * part
        base = chunk * padded(part)

        @pl.loop(0, part // STRIP)
        def _(strip):
            row = pl.multiple_of(strip * STRIP, STRIP)
            x = x_ref[pl.ds(start + row, STRIP), :].astype(jnp.float32)
            peak = jnp.max(x, axis=1, keepdims=True)
            x = x - peak
            record = jnp.where(lane == 0, peak, 0.0)
            for k in range(heats):
                total = jnp.sum(jnp.exp2(x * inverse_ref[k]), axis=1, keepdims=True)
                record = jnp.where(lane == k + 1, total, record)
            column[pl.ds(base + row, STRIP), :] = record

    out_ref[...] = column[...].T[: out_ref.shape[0], :]


def local_stats(values, pieces, inverse):
    tokens, heats = values[0].shape[0] // pieces, inverse.shape[0]
    lanes = len(values) * pieces * padded(tokens)
    size = len(values) * values[0].size
    return pl.pallas_call(
        functools.partial(stats_kernel, heats, pieces),
        out_shape=jax.ShapeDtypeStruct((8, lanes), jnp.float32),
        in_specs=[SMEM] + [VMEM] * len(values),
        out_specs=VMEM,
        scratch_shapes=[pltpu.VMEM((lanes, LANES), jnp.float32)],
        compiler_params=pltpu.CompilerParams(vmem_limit_bytes=4 << 20),
        cost_estimate=pl.CostEstimate(flops=2 * heats * size, bytes_accessed=2 * size, transcendentals=heats * size),
        name="stats",
    )(inverse, *values)


def grad_kernel(heats, pieces, scalars_ref, teacher_ref, *refs):
    values, stats, (out_ref, column) = refs[: len(pieces)], refs[len(pieces) : -2], refs[-2:]
    width = teacher_ref.shape[1]
    lane = lax.broadcasted_iota(jnp.int32, (STRIP, width), 1).astype(jnp.float32)
    done = 0
    for x_ref, stats_ref, (start, token, count) in zip(values, stats, pieces):
        column[...] = stats_ref[...].T
        base = done

        @pl.loop(0, count // STRIP)
        def _(strip):
            row = pl.multiple_of(strip * STRIP, STRIP)
            record = column[pl.ds(start + row, STRIP), :]
            x = x_ref[pl.ds(start + row, STRIP), :] - record[:, 0:1]
            t = teacher_ref[pl.ds(token + row, STRIP), :].astype(jnp.float32) - record[:, 8:9]
            result = jnp.exp2(x * scalars_ref[0, 0]) * (scalars_ref[1, 0] / record[:, 1:2])
            result = result - jnp.where(lane == record[:, 15:16], scalars_ref[1, 0], 0.0)
            for k in range(1, heats + 1):
                scale, factor = scalars_ref[0, k], scalars_ref[1, k]
                result = result + jnp.exp2(x * scale) * (factor / record[:, k + 1 : k + 2])
                result = result - jnp.exp2(t * scale) * (factor / record[:, k + 8 : k + 9])
            out_ref[pl.ds(base + row, STRIP), :] = result.astype(out_ref.dtype)

        done += count


def logit_grad(first, last, logits, teacher, stats, scalars):
    heats = scalars.shape[1] - 1
    part, width = logits[0].shape
    pieces, values, records = [], [], []
    for c in range(len(logits)):
        low, high = max(first, c * part), min(last, (c + 1) * part)
        if low < high:
            pieces.append((low - c * part, low, high - low))
            values.append(logits[c])
            records.append(stats[c])
    size = (last - first) * width
    return pl.pallas_call(
        functools.partial(grad_kernel, heats, pieces),
        out_shape=jax.ShapeDtypeStruct((last - first, width), jnp.bfloat16),
        in_specs=[SMEM] + [VMEM] * (1 + 2 * len(pieces)),
        out_specs=VMEM,
        scratch_shapes=[pltpu.VMEM((padded(part), stats[0].shape[0]), jnp.float32)],
        compiler_params=pltpu.CompilerParams(vmem_limit_bytes=4 << 20),
        cost_estimate=pl.CostEstimate(
            flops=6 * heats * size, bytes_accessed=8 * size, transcendentals=2 * heats * size
        ),
        name="grad",
    )(scalars, teacher, *values, *records)


def merge(mine, other, inverse):
    heats = inverse.shape[0]
    highest = jnp.maximum(mine[0:1], other[0:1])
    total = mine[1 : heats + 1] * jnp.exp2((mine[0:1] - highest) * inverse) + other[1 : heats + 1] * jnp.exp2(
        (other[0:1] - highest) * inverse
    )
    return jnp.concatenate([highest, total, mine[heats + 1 :]], axis=0)


def copy_kernel(rows, order_ref, in_ref, *refs):
    *out_refs, held, come, gone = refs
    inward, outward = [], []
    for side, out_ref in enumerate(out_refs):
        for k in range(out_ref.shape[0]):
            start = pl.multiple_of(order_ref[side, k] * rows, rows)
            slot = side * out_ref.shape[0] + k
            inward.append(pltpu.make_async_copy(in_ref.at[pl.ds(start, rows)], held.at[slot], come.at[slot]))
            outward.append(pltpu.make_async_copy(held.at[slot], out_ref.at[k], gone.at[slot]))
    for copy in inward:
        copy.start()
    for come_copy, gone_copy in zip(inward, outward):
        come_copy.wait()
        gone_copy.start()
    for copy in outward:
        copy.wait()


def row_blocks(array, order, rows):
    sides, count = order.shape
    block = jax.ShapeDtypeStruct((count, rows, array.shape[1]), array.dtype)
    hbm = pl.BlockSpec(memory_space=pltpu.HBM)
    return pl.pallas_call(
        functools.partial(copy_kernel, rows),
        out_shape=[block] * sides,
        in_specs=[SMEM, hbm],
        out_specs=[hbm] * sides,
        scratch_shapes=[
            pltpu.VMEM((sides * count, rows, array.shape[1]), array.dtype),
            pltpu.SemaphoreType.DMA((sides * count,)),
            pltpu.SemaphoreType.DMA((sides * count,)),
        ],
        compiler_params=pltpu.CompilerParams(vmem_limit_bytes=8 << 20),
        cost_estimate=pl.CostEstimate(flops=0, bytes_accessed=4 * array.size, transcendentals=0),
        name="row_blocks",
    )(order, array)


def shards(hidden_t, head, teacher, labels, temps, mix):
    count_dp, count_vocab = lax.axis_size("dp"), lax.axis_size("vocab")
    me_dp, me_vocab = lax.axis_index("dp"), lax.axis_index("vocab")
    rows = hidden_t.shape[0]
    tokens, width = teacher.shape
    part = tokens // CHUNKS
    heats = temps.shape[0]
    far = list(masks_far_first(count_vocab))
    near = far[::-1]
    dp_masks = list(masks_far_first(count_dp))

    own = hidden_t.T.reshape(count_dp, CHUNKS, part, rows).transpose(1, 0, 2, 3).reshape(-1, rows)

    inverse = LOG2E / temps
    weights = mix[1] * temps
    student_inverse = jnp.concatenate([jnp.full((1,), LOG2E, jnp.float32), inverse])
    scalars = jnp.stack([student_inverse, jnp.concatenate([mix[:1], weights])])
    relative = jnp.arange(0, count_vocab, 2, dtype=jnp.int32)
    keep_order = me_vocab ^ relative
    send_order = me_vocab ^ (relative + 1)

    def partial_logits(gathered):
        partial = jnp.dot(gathered, head, preferred_element_type=jnp.float32)
        return partial.reshape(*[2] * len(dp_masks), part, width)

    def reduced(partial, masks):
        left = dp_masks
        for mask in masks:
            axis, bit = left.index(mask), (me_dp // mask) % 2
            other = swap(pick(partial, 1 - bit, axis).astype(jnp.float16), "dp", mask)
            partial = pick(partial, bit, axis) + other.astype(jnp.float32)
            left = [m for m in left if m != mask]
        return partial

    def merged(student, fixed):
        stats = jnp.concatenate([student, fixed])
        for mask in near:
            other = swap(stats, "vocab", mask)
            stats = jnp.concatenate(
                [
                    merge(stats[:8], other[:8], student_inverse[:, None]),
                    merge(stats[8:], other[8:], inverse[:, None]),
                ]
            )
        return stats

    def products(blocks, grad):
        return lax.dot_general(blocks, grad, (((2,), (1,)), ((), ())), preferred_element_type=jnp.float32)

    def folded(blocks, mask):
        sent = [k for k in sorted(blocks) if k & mask]
        other = swap(jnp.stack([blocks[k].astype(jnp.bfloat16) for k in sent]), "vocab", mask)
        return {k ^ mask: blocks[k ^ mask] + other[n].astype(jnp.float32) for n, k in enumerate(sent)}

    def split(blocks):
        return [{k: blocks[k][: rows // 2] for k in blocks}, {k: blocks[k][rows // 2 :] for k in blocks}]

    def both(sides, masks):
        return [folded(side, mask) for side, mask in zip(sides, masks)]

    have, cross = [], []
    for c in range(CHUNKS):
        block = own[c * count_dp * part : (c + 1) * count_dp * part][None]
        have.append({0: block})
        cross.append({1: swap(block, "vocab", 1)})
    own_stats = local_stats([teacher], CHUNKS, inverse)
    for step in range(len(far) - 1):
        arrived = []
        for c in range(CHUNKS):
            mask = far[:-1][step] if c % 2 else near[1:][step]
            keys = sorted(have[c])
            arrived.append((keys, mask, swap(jnp.concatenate([have[c][k] for k in keys]), "vocab", mask)))
        for c, (keys, mask, other) in enumerate(arrived):
            other_cross = swap(other, "vocab", 1)
            for place, k in enumerate(keys):
                have[c][k ^ mask] = other[place : place + 1]
                cross[c][k ^ mask ^ 1] = other_cross[place : place + 1]
        if step == 0:
            own_stats, have = lax.optimization_barrier((own_stats, have))
            head_send, head_keep = row_blocks(head, jnp.stack([send_order, keep_order]), rows)

    (head_send, head_keep), have, cross = lax.optimization_barrier(((head_send, head_keep), have, cross))
    gathered, partials = [], []
    for c in range(CHUNKS):
        found = have[c] | cross[c]
        found = jnp.concatenate([found[k] for k in range(count_vocab)])
        gathered.append(jnp.concatenate([pick(found, me_vocab ^ n) for n in range(count_vocab)], axis=1))
        partials.append(partial_logits(gathered[c]))
    logits = [
        reduced(partials[c], dp_masks if c % 2 else dp_masks[::-1]) for c in range(CHUNKS)
    ]
    place = (labels - me_vocab * width).astype(jnp.float32).reshape(CHUNKS, part)
    place = jnp.pad(place, ((0, 0), (0, padded(part) - part))).reshape(1, -1)
    stats = merged(local_stats(logits, 1, student_inverse), own_stats)
    stats = jnp.split(jnp.concatenate([stats[:15], place]), CHUNKS, axis=1)

    cuts = [0, FIRST, tokens]
    grads, arrived = [], []
    for first, last in zip(cuts, cuts[1:]):
        if grads:
            grads[-1], logits = lax.optimization_barrier((grads[-1], logits))
        grads.append(logit_grad(first, last, logits, teacher, stats, scalars))
    arrived = [[swap(grad, "dp", r) for r in range(1, count_dp)] for grad in grads]

    def summed(c):
        found = jnp.stack([grads[c]] + arrived[c])
        grad_all = jnp.concatenate([pick(found, me_dp ^ n) for n in range(count_dp)])
        grad_all = lax.optimization_barrier(grad_all)
        crossed = swap(products(head_send, grad_all).astype(jnp.bfloat16), "vocab", 1)
        keep = products(head_keep, grad_all)
        return grad_all, {
            2 * k: keep[k] + crossed[k].astype(jnp.float32) for k in range(count_vocab // 2)
        }

    grads[1], arrived[0] = lax.optimization_barrier((grads[1], arrived[0]))
    arrived[1] = [swap(grads[1], "dp", r) for r in range(1, count_dp)]
    all_grads = [None, None]
    all_grads[0], early = summed(0)
    steps = list(zip(near[1:], far))
    early = split(early)
    for step in steps:
        early = both(early, step)
    arrived[1], early = lax.optimization_barrier((arrived[1], early))
    all_grads[1], late = summed(1)
    early, late, all_grads = lax.optimization_barrier((early, late, all_grads))
    head_grad = lax.dot_general(
        jnp.concatenate(gathered, axis=0),
        jnp.concatenate([g.reshape(count_dp, -1, width) for g in all_grads], axis=1)
        .reshape(count_dp, CHUNKS, part, width)
        .transpose(1, 0, 2, 3)
        .reshape(-1, width),
        (((0,), (0,)), ((), ())),
        preferred_element_type=jnp.float32,
    ).astype(jnp.bfloat16)
    late = split(late)
    for step in steps:
        late = both(late, step)
    hidden_parts = [jnp.concatenate([side[0] for side in sides]) for sides in (early, late)]
    hidden_grad = jnp.concatenate([p.reshape(rows, count_dp, -1) for p in hidden_parts], axis=2)
    return (hidden_grad.reshape(rows, count_dp * tokens), head_grad)


def solution(mesh):
    placed = (P(("dp", "vocab"), None), P("dp", "vocab"), P("dp", "vocab"), P("dp"), P(), P())
    return jax.shard_map(
        shards,
        mesh=mesh,
        in_specs=placed,
        out_specs=(P(("dp", "vocab"), None), P("dp", "vocab")),
        check_vma=False,
    )
```

```python
import functools

import jax
import jax.numpy as jnp
from jax import lax
from jax.experimental import pallas as pl
from jax.experimental.pallas import tpu as pltpu
from jax.sharding import PartitionSpec as P

CHUNKS = 2
FIRST = 96
STRIP = 32
LANES = 128
LOG2E = 1.4426950408889634


def swap(value, axis, mask):
    count = lax.axis_size(axis)
    return lax.ppermute(value, axis, [(k, k ^ mask) for k in range(count)])


def masks_far_first(count):
    mask = count // 2
    while mask:
        yield mask
        mask //= 2


def pick(parts, place, axis=0):
    return lax.dynamic_index_in_dim(parts, place, axis, keepdims=False)


def padded(count):
    return -(-count // LANES) * LANES


VMEM = pl.BlockSpec(memory_space=pltpu.VMEM)
SMEM = pl.BlockSpec(memory_space=pltpu.SMEM)


def stats_kernel(heats, pieces, inverse_ref, *refs):
    *values, out_ref, column = refs
    column[...] = jnp.zeros_like(column)
    lane = lax.broadcasted_iota(jnp.int32, (STRIP, LANES), 1)
    chunks = len(values) * pieces
    part = values[0].shape[0] // pieces
    for chunk in range(chunks):
        x_ref, start = values[chunk // pieces], chunk % pieces * part
        base = chunk * padded(part)

        @pl.loop(0, part // STRIP)
        def _(strip):
            row = pl.multiple_of(strip * STRIP, STRIP)
            x = x_ref[pl.ds(start + row, STRIP), :].astype(jnp.float32)
            peak = jnp.max(x, axis=1, keepdims=True)
            x = x - peak
            record = jnp.where(lane == 0, peak, 0.0)
            for k in range(heats):
                total = jnp.sum(jnp.exp2(x * inverse_ref[k]), axis=1, keepdims=True)
                record = jnp.where(lane == k + 1, total, record)
            column[pl.ds(base + row, STRIP), :] = record

    out_ref[...] = column[...].T[: out_ref.shape[0], :]


def local_stats(values, pieces, inverse):
    tokens, heats = values[0].shape[0] // pieces, inverse.shape[0]
    lanes = len(values) * pieces * padded(tokens)
    size = len(values) * values[0].size
    return pl.pallas_call(
        functools.partial(stats_kernel, heats, pieces),
        out_shape=jax.ShapeDtypeStruct((8, lanes), jnp.float32),
        in_specs=[SMEM] + [VMEM] * len(values),
        out_specs=VMEM,
        scratch_shapes=[pltpu.VMEM((lanes, LANES), jnp.float32)],
        compiler_params=pltpu.CompilerParams(vmem_limit_bytes=4 << 20),
        cost_estimate=pl.CostEstimate(flops=2 * heats * size, bytes_accessed=2 * size, transcendentals=heats * size),
        name="stats",
    )(inverse, *values)


def grad_kernel(heats, pieces, scalars_ref, teacher_ref, *refs):
    values, stats, (out_ref, column) = refs[: len(pieces)], refs[len(pieces) : -2], refs[-2:]
    width = teacher_ref.shape[1]
    lane = lax.broadcasted_iota(jnp.int32, (STRIP, width), 1).astype(jnp.float32)
    done = 0
    for x_ref, stats_ref, (start, token, count) in zip(values, stats, pieces):
        column[...] = stats_ref[...].T
        base = done

        @pl.loop(0, count // STRIP)
        def _(strip):
            row = pl.multiple_of(strip * STRIP, STRIP)
            record = column[pl.ds(start + row, STRIP), :]
            x = x_ref[pl.ds(start + row, STRIP), :] - record[:, 0:1]
            t = teacher_ref[pl.ds(token + row, STRIP), :].astype(jnp.float32) - record[:, 8:9]
            result = jnp.exp2(x * scalars_ref[0, 0]) * (scalars_ref[1, 0] / record[:, 1:2])
            result = result - jnp.where(lane == record[:, 15:16], scalars_ref[1, 0], 0.0)
            for k in range(1, heats + 1):
                scale, factor = scalars_ref[0, k], scalars_ref[1, k]
                result = result + jnp.exp2(x * scale) * (factor / record[:, k + 1 : k + 2])
                result = result - jnp.exp2(t * scale) * (factor / record[:, k + 8 : k + 9])
            out_ref[pl.ds(base + row, STRIP), :] = result.astype(out_ref.dtype)

        done += count


def logit_grad(first, last, logits, teacher, stats, scalars):
    heats = scalars.shape[1] - 1
    part, width = logits[0].shape
    pieces, values, records = [], [], []
    for c in range(len(logits)):
        low, high = max(first, c * part), min(last, (c + 1) * part)
        if low < high:
            pieces.append((low - c * part, low, high - low))
            values.append(logits[c])
            records.append(stats[c])
    size = (last - first) * width
    return pl.pallas_call(
        functools.partial(grad_kernel, heats, pieces),
        out_shape=jax.ShapeDtypeStruct((last - first, width), jnp.bfloat16),
        in_specs=[SMEM] + [VMEM] * (1 + 2 * len(pieces)),
        out_specs=VMEM,
        scratch_shapes=[pltpu.VMEM((padded(part), stats[0].shape[0]), jnp.float32)],
        compiler_params=pltpu.CompilerParams(vmem_limit_bytes=4 << 20),
        cost_estimate=pl.CostEstimate(
            flops=6 * heats * size, bytes_accessed=8 * size, transcendentals=2 * heats * size
        ),
        name="grad",
    )(scalars, teacher, *values, *records)


def merge(mine, other, inverse):
    heats = inverse.shape[0]
    highest = jnp.maximum(mine[0:1], other[0:1])
    total = mine[1 : heats + 1] * jnp.exp2((mine[0:1] - highest) * inverse) + other[1 : heats + 1] * jnp.exp2(
        (other[0:1] - highest) * inverse
    )
    return jnp.concatenate([highest, total, mine[heats + 1 :]], axis=0)


def copy_kernel(rows, order_ref, in_ref, *refs):
    *out_refs, held, come, gone = refs
    inward, outward = [], []
    for side, out_ref in enumerate(out_refs):
        for k in range(out_ref.shape[0]):
            start = pl.multiple_of(order_ref[side, k] * rows, rows)
            slot = side * out_ref.shape[0] + k
            inward.append(pltpu.make_async_copy(in_ref.at[pl.ds(start, rows)], held.at[slot], come.at[slot]))
            outward.append(pltpu.make_async_copy(held.at[slot], out_ref.at[k], gone.at[slot]))
    for copy in inward:
        copy.start()
    for come_copy, gone_copy in zip(inward, outward):
        come_copy.wait()
        gone_copy.start()
    for copy in outward:
        copy.wait()


def row_blocks(array, order, rows):
    sides, count = order.shape
    block = jax.ShapeDtypeStruct((count, rows, array.shape[1]), array.dtype)
    hbm = pl.BlockSpec(memory_space=pltpu.HBM)
    return pl.pallas_call(
        functools.partial(copy_kernel, rows),
        out_shape=[block] * sides,
        in_specs=[SMEM, hbm],
        out_specs=[hbm] * sides,
        scratch_shapes=[
            pltpu.VMEM((sides * count, rows, array.shape[1]), array.dtype),
            pltpu.SemaphoreType.DMA((sides * count,)),
            pltpu.SemaphoreType.DMA((sides * count,)),
        ],
        compiler_params=pltpu.CompilerParams(vmem_limit_bytes=8 << 20),
        cost_estimate=pl.CostEstimate(flops=0, bytes_accessed=4 * array.size, transcendentals=0),
        name="row_blocks",
    )(order, array)


def shards(hidden_t, head, teacher, labels, temps, mix):
    count_dp, count_vocab = lax.axis_size("dp"), lax.axis_size("vocab")
    me_dp, me_vocab = lax.axis_index("dp"), lax.axis_index("vocab")
    rows = hidden_t.shape[0]
    tokens, width = teacher.shape
    part = tokens // CHUNKS
    heats = temps.shape[0]
    far = list(masks_far_first(count_vocab))
    near = far[::-1]
    dp_masks = list(masks_far_first(count_dp))

    own = hidden_t.T.reshape(count_dp, CHUNKS, part, rows).transpose(1, 0, 2, 3).reshape(-1, rows)

    inverse = LOG2E / temps
    weights = mix[1] * temps
    student_inverse = jnp.concatenate([jnp.full((1,), LOG2E, jnp.float32), inverse])
    scalars = jnp.stack([student_inverse, jnp.concatenate([mix[:1], weights])])
    relative = jnp.arange(0, count_vocab, 2, dtype=jnp.int32)
    keep_order = me_vocab ^ relative
    send_order = me_vocab ^ (relative + 1)

    def partial_logits(gathered):
        partial = jnp.dot(gathered, head, preferred_element_type=jnp.float32)
        return partial.reshape(*[2] * len(dp_masks), part, width)

    def reduced(partial, masks):
        left = dp_masks
        for mask in masks:
            axis, bit = left.index(mask), (me_dp // mask) % 2
            other = swap(pick(partial, 1 - bit, axis).astype(jnp.float16), "dp", mask)
            partial = pick(partial, bit, axis) + other.astype(jnp.float32)
            left = [m for m in left if m != mask]
        return partial

    def merged(student, fixed):
        stats = jnp.concatenate([student, fixed])
        for mask in near:
            other = swap(stats, "vocab", mask)
            stats = jnp.concatenate(
                [
                    merge(stats[:8], other[:8], student_inverse[:, None]),
                    merge(stats[8:], other[8:], inverse[:, None]),
                ]
            )
        return stats

    def products(blocks, grad):
        return lax.dot_general(blocks, grad, (((2,), (1,)), ((), ())), preferred_element_type=jnp.float32)

    def folded(sides, masks):
        sent = [[k for k in sorted(side) if k & mask] for side, mask in zip(sides, masks)]
        others = [
            swap(jnp.stack([side[k].astype(jnp.bfloat16) for k in keys]), "vocab", mask)
            for side, keys, mask in zip(sides, sent, masks)
        ]
        others = lax.optimization_barrier(others)
        return [
            {k ^ mask: side[k ^ mask] + other[n].astype(jnp.float32) for n, k in enumerate(keys)}
            for side, keys, mask, other in zip(sides, sent, masks, others)
        ]

    def split(blocks):
        return [{k: blocks[k][: rows // 2] for k in blocks}, {k: blocks[k][rows // 2 :] for k in blocks}]

    have, cross = [], []
    for c in range(CHUNKS):
        block = own[c * count_dp * part : (c + 1) * count_dp * part][None]
        have.append({0: block})
        cross.append({1: swap(block, "vocab", 1)})
    own_stats = local_stats([teacher], CHUNKS, inverse)
    for step in range(len(far) - 1):
        arrived = []
        for c in range(CHUNKS):
            mask = far[:-1][step] if c % 2 else near[1:][step]
            keys = sorted(have[c])
            arrived.append((keys, mask, swap(jnp.concatenate([have[c][k] for k in keys]), "vocab", mask)))
        for c, (keys, mask, other) in enumerate(arrived):
            other_cross = swap(other, "vocab", 1)
            for place, k in enumerate(keys):
                have[c][k ^ mask] = other[place : place + 1]
                cross[c][k ^ mask ^ 1] = other_cross[place : place + 1]
        if step == 0:
            own_stats, have = lax.optimization_barrier((own_stats, have))
            head_send, head_keep = row_blocks(head, jnp.stack([send_order, keep_order]), rows)

    (head_send, head_keep), have, cross = lax.optimization_barrier(((head_send, head_keep), have, cross))
    gathered, partials = [], []
    for c in range(CHUNKS):
        found = have[c] | cross[c]
        found = jnp.concatenate([found[k] for k in range(count_vocab)])
        gathered.append(jnp.concatenate([pick(found, me_vocab ^ n) for n in range(count_vocab)], axis=1))
        partials.append(partial_logits(gathered[c]))
    logits = [
        reduced(partials[c], dp_masks if c % 2 else dp_masks[::-1]) for c in range(CHUNKS)
    ]
    place = (labels - me_vocab * width).astype(jnp.float32).reshape(CHUNKS, part)
    place = jnp.pad(place, ((0, 0), (0, padded(part) - part))).reshape(1, -1)
    stats = merged(local_stats(logits, 1, student_inverse), own_stats)
    stats = jnp.split(jnp.concatenate([stats[:15], place]), CHUNKS, axis=1)

    cuts = [0, FIRST, tokens]
    grads, arrived = [], []
    for first, last in zip(cuts, cuts[1:]):
        if grads:
            grads[-1], logits = lax.optimization_barrier((grads[-1], logits))
        grads.append(logit_grad(first, last, logits, teacher, stats, scalars))

    def crossing(c):
        found = jnp.stack([grads[c]] + [arrived[c][r] for r in range(1, count_dp)])
        grad_all = jnp.concatenate([pick(found, me_dp ^ n) for n in range(count_dp)])
        grad_all = lax.optimization_barrier(grad_all)
        crossed = swap(products(head_send, grad_all).astype(jnp.bfloat16), "vocab", 1)
        return crossed, grad_all

    def kept(crossed, grad_all):
        keep = products(head_keep, grad_all)
        return {2 * k: keep[k] + crossed[k].astype(jnp.float32) for k in range(count_vocab // 2)}

    arrived = [None, None]
    exchange = lambda grad: {r: swap(grad, "dp", r) for r in range(1, count_dp)}
    arrived[0] = exchange(grads[0])
    grads[1], arrived[0] = lax.optimization_barrier((grads[1], arrived[0]))
    arrived[1] = exchange(grads[1])
    steps = list(zip(near[1:], far))
    all_grads = [None, None]
    crossed, all_grads[0] = crossing(0)
    early = kept(crossed, all_grads[0])
    early, arrived[1][1] = lax.optimization_barrier((early, arrived[1][1]))
    early = split(early)
    early = folded(early, steps[0])
    crossed, all_grads[1] = crossing(1)
    late = kept(crossed, all_grads[1])
    early, late, all_grads = lax.optimization_barrier((early, late, all_grads))
    for step in steps[1:]:
        early = folded(early, step)
    head_grad = lax.dot_general(
        jnp.concatenate(gathered, axis=0),
        jnp.concatenate([g.reshape(count_dp, -1, width) for g in all_grads], axis=1)
        .reshape(count_dp, CHUNKS, part, width)
        .transpose(1, 0, 2, 3)
        .reshape(-1, width),
        (((0,), (0,)), ((), ())),
        preferred_element_type=jnp.float32,
    ).astype(jnp.bfloat16)
    late = split(late)
    for step in steps:
        late = folded(late, step)
    hidden_parts = [jnp.concatenate([side[0] for side in sides]) for sides in (early, late)]
    hidden_grad = jnp.concatenate([p.reshape(rows, count_dp, -1) for p in hidden_parts], axis=2)
    return (hidden_grad.reshape(rows, count_dp * tokens), head_grad)


def solution(mesh):
    placed = (P(("dp", "vocab"), None), P("dp", "vocab"), P("dp", "vocab"), P("dp"), P(), P())
    return jax.shard_map(
        shards,
        mesh=mesh,
        in_specs=placed,
        out_specs=(P(("dp", "vocab"), None), P("dp", "vocab")),
        check_vma=False,
    )
```

```python
import functools

import jax
import jax.numpy as jnp
from jax import lax
from jax.experimental import pallas as pl
from jax.experimental.pallas import tpu as pltpu
from jax.sharding import PartitionSpec as P

CHUNKS = 2
FIRST = 96
STRIP = 96
LANES = 128
LOG2E = 1.4426950408889634


def swap(value, axis, mask):
    count = lax.axis_size(axis)
    return lax.ppermute(value, axis, [(k, k ^ mask) for k in range(count)])


def masks_far_first(count):
    mask = count // 2
    while mask:
        yield mask
        mask //= 2


def pick(parts, place, axis=0):
    return lax.dynamic_index_in_dim(parts, place, axis, keepdims=False)


def padded(count):
    return -(-count // LANES) * LANES


VMEM = pl.BlockSpec(memory_space=pltpu.VMEM)
SMEM = pl.BlockSpec(memory_space=pltpu.SMEM)


def stats_kernel(heats, pieces, inverse_ref, *refs):
    *values, out_ref, column = refs
    column[...] = jnp.zeros_like(column)
    lane = lax.broadcasted_iota(jnp.int32, (STRIP, LANES), 1)
    chunks = len(values) * pieces
    part = values[0].shape[0] // pieces
    for chunk in range(chunks):
        x_ref, start = values[chunk // pieces], chunk % pieces * part
        base = chunk * padded(part)

        @pl.loop(0, part // STRIP)
        def _(strip):
            row = pl.multiple_of(strip * STRIP, STRIP)
            x = x_ref[pl.ds(start + row, STRIP), :].astype(jnp.float32)
            peak = jnp.max(x, axis=1, keepdims=True)
            x = x - peak
            record = jnp.where(lane == 0, peak, 0.0)
            for k in range(heats):
                total = jnp.sum(jnp.exp2(x * inverse_ref[k]), axis=1, keepdims=True)
                record = jnp.where(lane == k + 1, total, record)
            column[pl.ds(base + row, STRIP), :] = record

    out_ref[...] = column[...].T[: out_ref.shape[0], :]


def local_stats(values, pieces, inverse):
    tokens, heats = values[0].shape[0] // pieces, inverse.shape[0]
    lanes = len(values) * pieces * padded(tokens)
    size = len(values) * values[0].size
    return pl.pallas_call(
        functools.partial(stats_kernel, heats, pieces),
        out_shape=jax.ShapeDtypeStruct((8, lanes), jnp.float32),
        in_specs=[SMEM] + [VMEM] * len(values),
        out_specs=VMEM,
        scratch_shapes=[pltpu.VMEM((lanes, LANES), jnp.float32)],
        compiler_params=pltpu.CompilerParams(vmem_limit_bytes=4 << 20),
        cost_estimate=pl.CostEstimate(flops=2 * heats * size, bytes_accessed=2 * size, transcendentals=heats * size),
        name="stats",
    )(inverse, *values)


def grad_kernel(heats, pieces, scalars_ref, teacher_ref, *refs):
    values, stats, (out_ref, column) = refs[: len(pieces)], refs[len(pieces) : -2], refs[-2:]
    width = teacher_ref.shape[1]
    lane = lax.broadcasted_iota(jnp.int32, (STRIP, width), 1).astype(jnp.float32)
    done = 0
    for x_ref, stats_ref, (start, token, count) in zip(values, stats, pieces):
        column[...] = stats_ref[...].T
        base = done

        @pl.loop(0, count // STRIP)
        def _(strip):
            row = pl.multiple_of(strip * STRIP, STRIP)
            record = column[pl.ds(start + row, STRIP), :]
            x = x_ref[pl.ds(start + row, STRIP), :] - record[:, 0:1]
            t = teacher_ref[pl.ds(token + row, STRIP), :].astype(jnp.float32) - record[:, 8:9]
            result = jnp.exp2(x * scalars_ref[0, 0]) * (scalars_ref[1, 0] / record[:, 1:2])
            result = result - jnp.where(lane == record[:, 15:16], scalars_ref[1, 0], 0.0)
            for k in range(1, heats + 1):
                scale, factor = scalars_ref[0, k], scalars_ref[1, k]
                result = result + jnp.exp2(x * scale) * (factor / record[:, k + 1 : k + 2])
                result = result - jnp.exp2(t * scale) * (factor / record[:, k + 8 : k + 9])
            out_ref[pl.ds(base + row, STRIP), :] = result.astype(out_ref.dtype)

        done += count


def logit_grad(first, last, logits, teacher, stats, scalars):
    heats = scalars.shape[1] - 1
    part, width = logits[0].shape
    pieces, values, records = [], [], []
    for c in range(len(logits)):
        low, high = max(first, c * part), min(last, (c + 1) * part)
        if low < high:
            pieces.append((low - c * part, low, high - low))
            values.append(logits[c])
            records.append(stats[c])
    size = (last - first) * width
    return pl.pallas_call(
        functools.partial(grad_kernel, heats, pieces),
        out_shape=jax.ShapeDtypeStruct((last - first, width), jnp.bfloat16),
        in_specs=[SMEM] + [VMEM] * (1 + 2 * len(pieces)),
        out_specs=VMEM,
        scratch_shapes=[pltpu.VMEM((padded(part), stats[0].shape[0]), jnp.float32)],
        compiler_params=pltpu.CompilerParams(vmem_limit_bytes=4 << 20),
        cost_estimate=pl.CostEstimate(
            flops=6 * heats * size, bytes_accessed=8 * size, transcendentals=2 * heats * size
        ),
        name="grad",
    )(scalars, teacher, *values, *records)


def merge(mine, other, inverse):
    heats = inverse.shape[0]
    highest = jnp.maximum(mine[0:1], other[0:1])
    total = mine[1 : heats + 1] * jnp.exp2((mine[0:1] - highest) * inverse) + other[1 : heats + 1] * jnp.exp2(
        (other[0:1] - highest) * inverse
    )
    return jnp.concatenate([highest, total, mine[heats + 1 :]], axis=0)


def copy_kernel(rows, order_ref, in_ref, *refs):
    *out_refs, held, come, gone = refs
    inward, outward = [], []
    for side, out_ref in enumerate(out_refs):
        for k in range(out_ref.shape[0]):
            start = pl.multiple_of(order_ref[side, k] * rows, rows)
            slot = side * out_ref.shape[0] + k
            inward.append(pltpu.make_async_copy(in_ref.at[pl.ds(start, rows)], held.at[slot], come.at[slot]))
            outward.append(pltpu.make_async_copy(held.at[slot], out_ref.at[k], gone.at[slot]))
    for copy in inward:
        copy.start()
    for come_copy, gone_copy in zip(inward, outward):
        come_copy.wait()
        gone_copy.start()
    for copy in outward:
        copy.wait()


def row_blocks(array, order, rows):
    sides, count = order.shape
    block = jax.ShapeDtypeStruct((count, rows, array.shape[1]), array.dtype)
    hbm = pl.BlockSpec(memory_space=pltpu.HBM)
    return pl.pallas_call(
        functools.partial(copy_kernel, rows),
        out_shape=[block] * sides,
        in_specs=[SMEM, hbm],
        out_specs=[hbm] * sides,
        scratch_shapes=[
            pltpu.VMEM((sides * count, rows, array.shape[1]), array.dtype),
            pltpu.SemaphoreType.DMA((sides * count,)),
            pltpu.SemaphoreType.DMA((sides * count,)),
        ],
        compiler_params=pltpu.CompilerParams(vmem_limit_bytes=8 << 20),
        cost_estimate=pl.CostEstimate(flops=0, bytes_accessed=4 * array.size, transcendentals=0),
        name="row_blocks",
    )(order, array)


def shards(hidden_t, head, teacher, labels, temps, mix):
    count_dp, count_vocab = lax.axis_size("dp"), lax.axis_size("vocab")
    me_dp, me_vocab = lax.axis_index("dp"), lax.axis_index("vocab")
    rows = hidden_t.shape[0]
    tokens, width = teacher.shape
    part = tokens // CHUNKS
    heats = temps.shape[0]
    far = list(masks_far_first(count_vocab))
    near = far[::-1]
    dp_masks = list(masks_far_first(count_dp))

    own = hidden_t.T.reshape(count_dp, CHUNKS, part, rows).transpose(1, 0, 2, 3).reshape(-1, rows)

    inverse = LOG2E / temps
    weights = mix[1] * temps
    student_inverse = jnp.concatenate([jnp.full((1,), LOG2E, jnp.float32), inverse])
    scalars = jnp.stack([student_inverse, jnp.concatenate([mix[:1], weights])])
    relative = jnp.arange(0, count_vocab, 2, dtype=jnp.int32)
    keep_order = me_vocab ^ relative
    send_order = me_vocab ^ (relative + 1)

    def partial_logits(gathered):
        partial = jnp.dot(gathered, head, preferred_element_type=jnp.float32)
        return partial.reshape(*[2] * len(dp_masks), part, width)

    def reduced(partial, masks):
        left = dp_masks
        for mask in masks:
            axis, bit = left.index(mask), (me_dp // mask) % 2
            other = swap(pick(partial, 1 - bit, axis).astype(jnp.float16), "dp", mask)
            partial = pick(partial, bit, axis) + other.astype(jnp.float32)
            left = [m for m in left if m != mask]
        return partial

    def merged(student, fixed):
        stats = jnp.concatenate([student, fixed])
        for mask in near:
            other = swap(stats, "vocab", mask)
            stats = jnp.concatenate(
                [
                    merge(stats[:8], other[:8], student_inverse[:, None]),
                    merge(stats[8:], other[8:], inverse[:, None]),
                ]
            )
        return stats

    def products(blocks, grad):
        return lax.dot_general(blocks, grad, (((2,), (1,)), ((), ())), preferred_element_type=jnp.float32)

    def folded(sides, masks):
        sent = [[k for k in sorted(side) if k & mask] for side, mask in zip(sides, masks)]
        others = [
            swap(jnp.stack([side[k].astype(jnp.bfloat16) for k in keys]), "vocab", mask)
            for side, keys, mask in zip(sides, sent, masks)
        ]
        others = lax.optimization_barrier(others)
        return [
            {k ^ mask: side[k ^ mask] + other[n].astype(jnp.float32) for n, k in enumerate(keys)}
            for side, keys, mask, other in zip(sides, sent, masks, others)
        ]

    def split(blocks):
        return [{k: blocks[k][: rows // 2] for k in blocks}, {k: blocks[k][rows // 2 :] for k in blocks}]

    have, cross = [], []
    for c in range(CHUNKS):
        block = own[c * count_dp * part : (c + 1) * count_dp * part][None]
        have.append({0: block})
        cross.append({1: swap(block, "vocab", 1)})
    own_stats = local_stats([teacher], CHUNKS, inverse)
    for step in range(len(far) - 1):
        arrived = []
        for c in range(CHUNKS):
            mask = far[:-1][step] if c % 2 else near[1:][step]
            keys = sorted(have[c])
            arrived.append((keys, mask, swap(jnp.concatenate([have[c][k] for k in keys]), "vocab", mask)))
        for c, (keys, mask, other) in enumerate(arrived):
            other_cross = swap(other, "vocab", 1)
            for place, k in enumerate(keys):
                have[c][k ^ mask] = other[place : place + 1]
                cross[c][k ^ mask ^ 1] = other_cross[place : place + 1]
        if step == 0:
            own_stats, have = lax.optimization_barrier((own_stats, have))
            head_send, head_keep = row_blocks(head, jnp.stack([send_order, keep_order]), rows)

    (head_send, head_keep), have, cross = lax.optimization_barrier(((head_send, head_keep), have, cross))
    gathered, partials = [], []
    for c in range(CHUNKS):
        found = have[c] | cross[c]
        found = jnp.concatenate([found[k] for k in range(count_vocab)])
        gathered.append(jnp.concatenate([pick(found, me_vocab ^ n) for n in range(count_vocab)], axis=1))
        partials.append(partial_logits(gathered[c]))
    logits = [
        reduced(partials[c], dp_masks if c % 2 else dp_masks[::-1]) for c in range(CHUNKS)
    ]
    place = (labels - me_vocab * width).astype(jnp.float32).reshape(CHUNKS, part)
    place = jnp.pad(place, ((0, 0), (0, padded(part) - part))).reshape(1, -1)
    stats = merged(local_stats(logits, 1, student_inverse), own_stats)
    stats = jnp.split(jnp.concatenate([stats[:15], place]), CHUNKS, axis=1)

    cuts = [0, FIRST, tokens]
    grads, arrived = [], []
    for first, last in zip(cuts, cuts[1:]):
        if grads:
            grads[-1], logits = lax.optimization_barrier((grads[-1], logits))
        grads.append(logit_grad(first, last, logits, teacher, stats, scalars))

    def crossing(c):
        found = jnp.stack([grads[c]] + [arrived[c][r] for r in range(1, count_dp)])
        grad_all = jnp.concatenate([pick(found, me_dp ^ n) for n in range(count_dp)])
        grad_all = lax.optimization_barrier(grad_all)
        crossed = swap(products(head_send, grad_all).astype(jnp.bfloat16), "vocab", 1)
        return crossed, grad_all

    def kept(crossed, grad_all):
        keep = products(head_keep, grad_all)
        return {2 * k: keep[k] + crossed[k].astype(jnp.float32) for k in range(count_vocab // 2)}

    arrived = [None, None]
    exchange = lambda grad: {r: swap(grad, "dp", r) for r in range(1, count_dp)}
    arrived[0] = exchange(grads[0])
    grads[1], arrived[0] = lax.optimization_barrier((grads[1], arrived[0]))
    arrived[1] = exchange(grads[1])
    steps = list(zip(near[1:], far))
    all_grads = [None, None]
    crossed, all_grads[0] = crossing(0)
    early = kept(crossed, all_grads[0])
    early, arrived[1][1] = lax.optimization_barrier((early, arrived[1][1]))
    early = split(early)
    early = folded(early, steps[0])
    crossed, all_grads[1] = crossing(1)
    late = kept(crossed, all_grads[1])
    early, late, all_grads = lax.optimization_barrier((early, late, all_grads))
    for step in steps[1:]:
        early = folded(early, step)
    head_grad = lax.dot_general(
        jnp.concatenate(gathered, axis=0),
        jnp.concatenate([g.reshape(count_dp, -1, width) for g in all_grads], axis=1)
        .reshape(count_dp, CHUNKS, part, width)
        .transpose(1, 0, 2, 3)
        .reshape(-1, width),
        (((0,), (0,)), ((), ())),
        preferred_element_type=jnp.float32,
    ).astype(jnp.bfloat16)
    late = split(late)
    for step in steps:
        late = folded(late, step)
    hidden_parts = [jnp.concatenate([side[0] for side in sides]) for sides in (early, late)]
    hidden_grad = jnp.concatenate([p.reshape(rows, count_dp, -1) for p in hidden_parts], axis=2)
    return (hidden_grad.reshape(rows, count_dp * tokens), head_grad)


def solution(mesh):
    placed = (P(("dp", "vocab"), None), P("dp", "vocab"), P("dp", "vocab"), P("dp"), P(), P())
    return jax.shard_map(
        shards,
        mesh=mesh,
        in_specs=placed,
        out_specs=(P(("dp", "vocab"), None), P("dp", "vocab")),
        check_vma=False,
    )
```

```python
import functools

import jax
import jax.numpy as jnp
from jax import lax
from jax.experimental import pallas as pl
from jax.experimental.pallas import tpu as pltpu
from jax.sharding import PartitionSpec as P

CHUNKS = 2
FIRST = 96
STRIP = 96
LANES = 128
LOG2E = 1.4426950408889634


def swap(value, axis, mask):
    count = lax.axis_size(axis)
    return lax.ppermute(value, axis, [(k, k ^ mask) for k in range(count)])


def masks_far_first(count):
    mask = count // 2
    while mask:
        yield mask
        mask //= 2


def pick(parts, place, axis=0):
    return lax.dynamic_index_in_dim(parts, place, axis, keepdims=False)


def padded(count):
    return -(-count // LANES) * LANES


VMEM = pl.BlockSpec(memory_space=pltpu.VMEM)
SMEM = pl.BlockSpec(memory_space=pltpu.SMEM)


def stats_kernel(heats, pieces, inverse_ref, *refs):
    *values, out_ref, column = refs
    column[...] = jnp.zeros_like(column)
    lane = lax.broadcasted_iota(jnp.int32, (STRIP, LANES), 1)
    chunks = len(values) * pieces
    part = values[0].shape[0] // pieces
    for chunk in range(chunks):
        x_ref, start = values[chunk // pieces], chunk % pieces * part
        base = chunk * padded(part)

        @pl.loop(0, part // STRIP)
        def _(strip):
            row = pl.multiple_of(strip * STRIP, STRIP)
            x = x_ref[pl.ds(start + row, STRIP), :].astype(jnp.float32)
            peak = jnp.max(x, axis=1, keepdims=True)
            x = x - peak
            record = jnp.where(lane == 0, peak, 0.0)
            for k in range(heats):
                total = jnp.sum(jnp.exp2(x * inverse_ref[k]), axis=1, keepdims=True)
                record = jnp.where(lane == k + 1, total, record)
            column[pl.ds(base + row, STRIP), :] = record

    out_ref[...] = column[...].T[: out_ref.shape[0], :]


def local_stats(values, pieces, inverse):
    tokens, heats = values[0].shape[0] // pieces, inverse.shape[0]
    lanes = len(values) * pieces * padded(tokens)
    size = len(values) * values[0].size
    return pl.pallas_call(
        functools.partial(stats_kernel, heats, pieces),
        out_shape=jax.ShapeDtypeStruct((8, lanes), jnp.float32),
        in_specs=[SMEM] + [VMEM] * len(values),
        out_specs=VMEM,
        scratch_shapes=[pltpu.VMEM((lanes, LANES), jnp.float32)],
        compiler_params=pltpu.CompilerParams(vmem_limit_bytes=4 << 20),
        cost_estimate=pl.CostEstimate(flops=2 * heats * size, bytes_accessed=2 * size, transcendentals=heats * size),
        name="stats",
    )(inverse, *values)


def grad_kernel(heats, pieces, scalars_ref, teacher_ref, *refs):
    values, stats, (out_ref, column) = refs[: len(pieces)], refs[len(pieces) : -2], refs[-2:]
    width = teacher_ref.shape[1]
    lane = lax.broadcasted_iota(jnp.int32, (STRIP, width), 1).astype(jnp.float32)
    done = 0
    for x_ref, stats_ref, (start, token, count) in zip(values, stats, pieces):
        column[...] = stats_ref[...].T
        base = done

        @pl.loop(0, count // STRIP)
        def _(strip):
            row = pl.multiple_of(strip * STRIP, STRIP)
            record = column[pl.ds(start + row, STRIP), :]
            x = x_ref[pl.ds(start + row, STRIP), :] - record[:, 0:1]
            t = teacher_ref[pl.ds(token + row, STRIP), :].astype(jnp.float32) - record[:, 8:9]
            result = jnp.exp2(x * scalars_ref[0, 0]) * (scalars_ref[1, 0] / record[:, 1:2])
            result = result - jnp.where(lane == record[:, 15:16], scalars_ref[1, 0], 0.0)
            for k in range(1, heats + 1):
                scale, factor = scalars_ref[0, k], scalars_ref[1, k]
                result = result + jnp.exp2(x * scale) * (factor / record[:, k + 1 : k + 2])
                result = result - jnp.exp2(t * scale) * (factor / record[:, k + 8 : k + 9])
            out_ref[pl.ds(base + row, STRIP), :] = result.astype(out_ref.dtype)

        done += count


def logit_grad(first, last, logits, teacher, stats, scalars):
    heats = scalars.shape[1] - 1
    part, width = logits[0].shape
    pieces, values, records = [], [], []
    for c in range(len(logits)):
        low, high = max(first, c * part), min(last, (c + 1) * part)
        if low < high:
            pieces.append((low - c * part, low, high - low))
            values.append(logits[c])
            records.append(stats[c])
    size = (last - first) * width
    return pl.pallas_call(
        functools.partial(grad_kernel, heats, pieces),
        out_shape=jax.ShapeDtypeStruct((last - first, width), jnp.bfloat16),
        in_specs=[SMEM] + [VMEM] * (1 + 2 * len(pieces)),
        out_specs=VMEM,
        scratch_shapes=[pltpu.VMEM((padded(part), stats[0].shape[0]), jnp.float32)],
        compiler_params=pltpu.CompilerParams(vmem_limit_bytes=4 << 20),
        cost_estimate=pl.CostEstimate(
            flops=6 * heats * size, bytes_accessed=8 * size, transcendentals=2 * heats * size
        ),
        name="grad",
    )(scalars, teacher, *values, *records)


def merge(mine, other, inverse):
    heats = inverse.shape[0]
    highest = jnp.maximum(mine[0:1], other[0:1])
    total = mine[1 : heats + 1] * jnp.exp2((mine[0:1] - highest) * inverse) + other[1 : heats + 1] * jnp.exp2(
        (other[0:1] - highest) * inverse
    )
    return jnp.concatenate([highest, total, mine[heats + 1 :]], axis=0)


def copy_kernel(rows, order_ref, in_ref, *refs):
    *out_refs, held, come, gone = refs
    inward, outward = [], []
    for side, out_ref in enumerate(out_refs):
        for k in range(out_ref.shape[0]):
            start = pl.multiple_of(order_ref[side, k] * rows, rows)
            slot = side * out_ref.shape[0] + k
            inward.append(pltpu.make_async_copy(in_ref.at[pl.ds(start, rows)], held.at[slot], come.at[slot]))
            outward.append(pltpu.make_async_copy(held.at[slot], out_ref.at[k], gone.at[slot]))
    for copy in inward:
        copy.start()
    for come_copy, gone_copy in zip(inward, outward):
        come_copy.wait()
        gone_copy.start()
    for copy in outward:
        copy.wait()


def row_blocks(array, order, rows):
    sides, count = order.shape
    block = jax.ShapeDtypeStruct((count, rows, array.shape[1]), array.dtype)
    hbm = pl.BlockSpec(memory_space=pltpu.HBM)
    return pl.pallas_call(
        functools.partial(copy_kernel, rows),
        out_shape=[block] * sides,
        in_specs=[SMEM, hbm],
        out_specs=[hbm] * sides,
        scratch_shapes=[
            pltpu.VMEM((sides * count, rows, array.shape[1]), array.dtype),
            pltpu.SemaphoreType.DMA((sides * count,)),
            pltpu.SemaphoreType.DMA((sides * count,)),
        ],
        compiler_params=pltpu.CompilerParams(vmem_limit_bytes=8 << 20),
        cost_estimate=pl.CostEstimate(flops=0, bytes_accessed=4 * array.size, transcendentals=0),
        name="row_blocks",
    )(order, array)


def shards(hidden_t, head, teacher, labels, temps, mix):
    count_dp, count_vocab = lax.axis_size("dp"), lax.axis_size("vocab")
    me_dp, me_vocab = lax.axis_index("dp"), lax.axis_index("vocab")
    rows = hidden_t.shape[0]
    tokens, width = teacher.shape
    part = tokens // CHUNKS
    heats = temps.shape[0]
    far = list(masks_far_first(count_vocab))
    near = far[::-1]
    dp_masks = list(masks_far_first(count_dp))

    own = hidden_t.T.reshape(count_dp, CHUNKS, part, rows).transpose(1, 0, 2, 3).reshape(-1, rows)

    inverse = LOG2E / temps
    weights = mix[1] * temps
    student_inverse = jnp.concatenate([jnp.full((1,), LOG2E, jnp.float32), inverse])
    scalars = jnp.stack([student_inverse, jnp.concatenate([mix[:1], weights])])
    relative = jnp.arange(0, count_vocab, 2, dtype=jnp.int32)
    keep_order = me_vocab ^ relative
    send_order = me_vocab ^ (relative + 1)

    def partial_logits(gathered):
        partial = jnp.dot(gathered, head, preferred_element_type=jnp.float32)
        return partial.reshape(*[2] * len(dp_masks), part, width)

    def reduced(partial, masks):
        left = dp_masks
        for mask in masks:
            axis, bit = left.index(mask), (me_dp // mask) % 2
            other = swap(pick(partial, 1 - bit, axis).astype(jnp.float16), "dp", mask)
            partial = pick(partial, bit, axis) + other.astype(jnp.float32)
            left = [m for m in left if m != mask]
        return partial

    def merged(student, fixed):
        stats = jnp.concatenate([student, fixed])
        for mask in near:
            other = swap(stats, "vocab", mask)
            stats = jnp.concatenate(
                [
                    merge(stats[:8], other[:8], student_inverse[:, None]),
                    merge(stats[8:], other[8:], inverse[:, None]),
                ]
            )
        return stats

    def products(blocks, grad):
        return lax.dot_general(blocks, grad, (((2,), (1,)), ((), ())), preferred_element_type=jnp.float32)

    def folded(sides, masks):
        sent = [[k for k in sorted(side) if k & mask] for side, mask in zip(sides, masks)]
        others = [
            swap(jnp.stack([side[k].astype(jnp.bfloat16) for k in keys]), "vocab", mask)
            for side, keys, mask in zip(sides, sent, masks)
        ]
        others = lax.optimization_barrier(others)
        return [
            {k ^ mask: side[k ^ mask] + other[n].astype(jnp.float32) for n, k in enumerate(keys)}
            for side, keys, mask, other in zip(sides, sent, masks, others)
        ]

    def split(blocks):
        return [{k: blocks[k][: rows // 2] for k in blocks}, {k: blocks[k][rows // 2 :] for k in blocks}]

    have, cross = [], []
    for c in range(CHUNKS):
        block = own[c * count_dp * part : (c + 1) * count_dp * part][None]
        have.append({0: block})
        cross.append({1: swap(block, "vocab", 1)})
    own_stats = local_stats([teacher], CHUNKS, inverse)
    for step in range(len(far) - 1):
        arrived = []
        for c in range(CHUNKS):
            mask = far[:-1][step] if c % 2 else near[1:][step]
            keys = sorted(have[c])
            arrived.append((keys, mask, swap(jnp.concatenate([have[c][k] for k in keys]), "vocab", mask)))
        for c, (keys, mask, other) in enumerate(arrived):
            other_cross = swap(other, "vocab", 1)
            for place, k in enumerate(keys):
                have[c][k ^ mask] = other[place : place + 1]
                cross[c][k ^ mask ^ 1] = other_cross[place : place + 1]
        if step == 0:
            own_stats, have = lax.optimization_barrier((own_stats, have))
            head_send, head_keep = row_blocks(head, jnp.stack([send_order, keep_order]), rows)

    (head_send, head_keep), have, cross = lax.optimization_barrier(((head_send, head_keep), have, cross))
    gathered, partials = [], []
    for c in range(CHUNKS):
        found = have[c] | cross[c]
        found = jnp.concatenate([found[k] for k in range(count_vocab)])
        gathered.append(jnp.concatenate([pick(found, me_vocab ^ n) for n in range(count_vocab)], axis=1))
        partials.append(partial_logits(gathered[c]))
    logits = [
        reduced(partials[c], dp_masks if c % 2 else dp_masks[::-1]) for c in range(CHUNKS)
    ]
    place = (labels - me_vocab * width).astype(jnp.float32).reshape(CHUNKS, part)
    place = jnp.pad(place, ((0, 0), (0, padded(part) - part))).reshape(1, -1)
    stats = merged(local_stats(logits, 1, student_inverse), own_stats)
    stats = jnp.split(jnp.concatenate([stats[:15], place]), CHUNKS, axis=1)

    cuts = [0, FIRST, tokens]
    grads, arrived = [], []
    for first, last in zip(cuts, cuts[1:]):
        if grads:
            grads[-1], logits = lax.optimization_barrier((grads[-1], logits))
        grads.append(logit_grad(first, last, logits, teacher, stats, scalars))

    def crossing(c):
        arrived[c] = lax.optimization_barrier(arrived[c])
        found = jnp.stack([grads[c]] + [arrived[c][r] for r in range(1, count_dp)])
        grad_all = jnp.concatenate([pick(found, me_dp ^ n) for n in range(count_dp)])
        grad_all = lax.optimization_barrier(grad_all)
        crossed = swap(products(head_send, grad_all).astype(jnp.bfloat16), "vocab", 1)
        return crossed, grad_all

    def kept(crossed, grad_all):
        keep = products(head_keep, grad_all)
        return {2 * k: keep[k] + crossed[k].astype(jnp.float32) for k in range(count_vocab // 2)}

    arrived = [None, None]
    def exchange(grad):
        return {r: swap(grad, "dp", r) for r in range(1, count_dp)}

    arrived[0] = exchange(grads[0])
    grads[1], arrived[0] = lax.optimization_barrier((grads[1], arrived[0]))
    arrived[1] = exchange(grads[1])
    steps = list(zip(near[1:], far))
    all_grads = [None, None]
    crossed, all_grads[0] = crossing(0)
    early = kept(crossed, all_grads[0])
    early, arrived[1][1] = lax.optimization_barrier((early, arrived[1][1]))
    early = split(early)
    early = folded(early, steps[0])
    crossed, all_grads[1] = crossing(1)
    late = kept(crossed, all_grads[1])
    early, late, all_grads = lax.optimization_barrier((early, late, all_grads))
    for step in steps[1:]:
        early = folded(early, step)
    head_grad = lax.dot_general(
        jnp.concatenate(gathered, axis=0),
        jnp.concatenate([g.reshape(count_dp, -1, width) for g in all_grads], axis=1)
        .reshape(count_dp, CHUNKS, part, width)
        .transpose(1, 0, 2, 3)
        .reshape(-1, width),
        (((0,), (0,)), ((), ())),
        preferred_element_type=jnp.float32,
    ).astype(jnp.bfloat16)
    late = split(late)
    for step in steps:
        late = folded(late, step)
    hidden_parts = [jnp.concatenate([side[0] for side in sides]) for sides in (early, late)]
    hidden_grad = jnp.concatenate([p.reshape(rows, count_dp, -1) for p in hidden_parts], axis=2)
    return (hidden_grad.reshape(rows, count_dp * tokens), head_grad)


def solution(mesh):
    placed = (P(("dp", "vocab"), None), P("dp", "vocab"), P("dp", "vocab"), P("dp"), P(), P())
    return jax.shard_map(
        shards,
        mesh=mesh,
        in_specs=placed,
        out_specs=(P(("dp", "vocab"), None), P("dp", "vocab")),
        check_vma=False,
    )
```

```python
import functools

import jax
import jax.numpy as jnp
from jax import lax
from jax.experimental import pallas as pl
from jax.experimental.pallas import tpu as pltpu
from jax.sharding import PartitionSpec as P

CHUNKS = 2
FIRST = 96
STRIP = 96
LANES = 128
LOG2E = 1.4426950408889634


def swap(value, axis, mask):
    count = lax.axis_size(axis)
    return lax.ppermute(value, axis, [(k, k ^ mask) for k in range(count)])


def masks_far_first(count):
    mask = count // 2
    while mask:
        yield mask
        mask //= 2


def pick(parts, place, axis=0):
    return lax.dynamic_index_in_dim(parts, place, axis, keepdims=False)


def padded(count):
    return -(-count // LANES) * LANES


VMEM = pl.BlockSpec(memory_space=pltpu.VMEM)
SMEM = pl.BlockSpec(memory_space=pltpu.SMEM)


def stats_kernel(heats, pieces, inverse_ref, *refs):
    *values, out_ref, column = refs
    column[...] = jnp.zeros_like(column)
    lane = lax.broadcasted_iota(jnp.int32, (STRIP, LANES), 1)
    chunks = len(values) * pieces
    part = values[0].shape[0] // pieces
    for chunk in range(chunks):
        x_ref, start = values[chunk // pieces], chunk % pieces * part
        base = chunk * padded(part)

        @pl.loop(0, part // STRIP)
        def _(strip):
            row = pl.multiple_of(strip * STRIP, STRIP)
            x = x_ref[pl.ds(start + row, STRIP), :].astype(jnp.float32)
            peak = jnp.max(x, axis=1, keepdims=True)
            x = x - peak
            record = jnp.where(lane == 0, peak, 0.0)
            for k in range(heats):
                total = jnp.sum(jnp.exp2(x * inverse_ref[k]), axis=1, keepdims=True)
                record = jnp.where(lane == k + 1, total, record)
            column[pl.ds(base + row, STRIP), :] = record

    out_ref[...] = column[...].T[: out_ref.shape[0], :]


def local_stats(values, pieces, inverse):
    tokens, heats = values[0].shape[0] // pieces, inverse.shape[0]
    lanes = len(values) * pieces * padded(tokens)
    size = len(values) * values[0].size
    return pl.pallas_call(
        functools.partial(stats_kernel, heats, pieces),
        out_shape=jax.ShapeDtypeStruct((8, lanes), jnp.float32),
        in_specs=[SMEM] + [VMEM] * len(values),
        out_specs=VMEM,
        scratch_shapes=[pltpu.VMEM((lanes, LANES), jnp.float32)],
        compiler_params=pltpu.CompilerParams(vmem_limit_bytes=4 << 20),
        cost_estimate=pl.CostEstimate(flops=2 * heats * size, bytes_accessed=2 * size, transcendentals=heats * size),
        name="stats",
    )(inverse, *values)


def grad_kernel(heats, pieces, scalars_ref, teacher_ref, *refs):
    values, stats, (out_ref, column) = refs[: len(pieces)], refs[len(pieces) : -2], refs[-2:]
    width = teacher_ref.shape[1]
    lane = lax.broadcasted_iota(jnp.int32, (STRIP, width), 1).astype(jnp.float32)
    done = 0
    for x_ref, stats_ref, (start, token, count) in zip(values, stats, pieces):
        column[...] = stats_ref[...].T
        base = done

        @pl.loop(0, count // STRIP)
        def _(strip):
            row = pl.multiple_of(strip * STRIP, STRIP)
            record = column[pl.ds(start + row, STRIP), :]
            x = x_ref[pl.ds(start + row, STRIP), :] - record[:, 0:1]
            t = teacher_ref[pl.ds(token + row, STRIP), :].astype(jnp.float32) - record[:, 8:9]
            result = jnp.exp2(x * scalars_ref[0, 0]) * (scalars_ref[1, 0] / record[:, 1:2])
            result = result - jnp.where(lane == record[:, 15:16], scalars_ref[1, 0], 0.0)
            for k in range(1, heats + 1):
                scale, factor = scalars_ref[0, k], scalars_ref[1, k]
                result = result + jnp.exp2(x * scale) * (factor / record[:, k + 1 : k + 2])
                result = result - jnp.exp2(t * scale) * (factor / record[:, k + 8 : k + 9])
            out_ref[pl.ds(base + row, STRIP), :] = result.astype(out_ref.dtype)

        done += count


def logit_grad(first, last, logits, teacher, stats, scalars):
    heats = scalars.shape[1] - 1
    part, width = logits[0].shape
    pieces, values, records = [], [], []
    for c in range(len(logits)):
        low, high = max(first, c * part), min(last, (c + 1) * part)
        if low < high:
            pieces.append((low - c * part, low, high - low))
            values.append(logits[c])
            records.append(stats[c])
    size = (last - first) * width
    return pl.pallas_call(
        functools.partial(grad_kernel, heats, pieces),
        out_shape=jax.ShapeDtypeStruct((last - first, width), jnp.bfloat16),
        in_specs=[SMEM] + [VMEM] * (1 + 2 * len(pieces)),
        out_specs=VMEM,
        scratch_shapes=[pltpu.VMEM((padded(part), stats[0].shape[0]), jnp.float32)],
        compiler_params=pltpu.CompilerParams(vmem_limit_bytes=4 << 20),
        cost_estimate=pl.CostEstimate(
            flops=6 * heats * size, bytes_accessed=8 * size, transcendentals=2 * heats * size
        ),
        name="grad",
    )(scalars, teacher, *values, *records)


def merge(mine, other, inverse):
    heats = inverse.shape[0]
    highest = jnp.maximum(mine[0:1], other[0:1])
    total = mine[1 : heats + 1] * jnp.exp2((mine[0:1] - highest) * inverse) + other[1 : heats + 1] * jnp.exp2(
        (other[0:1] - highest) * inverse
    )
    return jnp.concatenate([highest, total, mine[heats + 1 :]], axis=0)


def copy_kernel(rows, order_ref, in_ref, *refs):
    *out_refs, held, come, gone = refs
    inward, outward = [], []
    for side, out_ref in enumerate(out_refs):
        for k in range(out_ref.shape[0]):
            start = pl.multiple_of(order_ref[side, k] * rows, rows)
            slot = side * out_ref.shape[0] + k
            inward.append(pltpu.make_async_copy(in_ref.at[pl.ds(start, rows)], held.at[slot], come.at[slot]))
            outward.append(pltpu.make_async_copy(held.at[slot], out_ref.at[k], gone.at[slot]))
    for copy in inward:
        copy.start()
    for come_copy, gone_copy in zip(inward, outward):
        come_copy.wait()
        gone_copy.start()
    for copy in outward:
        copy.wait()


def row_blocks(array, order, rows):
    sides, count = order.shape
    block = jax.ShapeDtypeStruct((count, rows, array.shape[1]), array.dtype)
    hbm = pl.BlockSpec(memory_space=pltpu.HBM)
    return pl.pallas_call(
        functools.partial(copy_kernel, rows),
        out_shape=[block] * sides,
        in_specs=[SMEM, hbm],
        out_specs=[hbm] * sides,
        scratch_shapes=[
            pltpu.VMEM((sides * count, rows, array.shape[1]), array.dtype),
            pltpu.SemaphoreType.DMA((sides * count,)),
            pltpu.SemaphoreType.DMA((sides * count,)),
        ],
        compiler_params=pltpu.CompilerParams(vmem_limit_bytes=8 << 20),
        cost_estimate=pl.CostEstimate(flops=0, bytes_accessed=4 * array.size, transcendentals=0),
        name="row_blocks",
    )(order, array)


def shards(hidden_t, head, teacher, labels, temps, mix):
    count_dp, count_vocab = lax.axis_size("dp"), lax.axis_size("vocab")
    me_dp, me_vocab = lax.axis_index("dp"), lax.axis_index("vocab")
    rows = hidden_t.shape[0]
    tokens, width = teacher.shape
    part = tokens // CHUNKS
    heats = temps.shape[0]
    far = list(masks_far_first(count_vocab))
    near = far[::-1]
    dp_masks = list(masks_far_first(count_dp))

    own = hidden_t.T.reshape(count_dp, CHUNKS, part, rows).transpose(1, 0, 2, 3).reshape(-1, rows)

    inverse = LOG2E / temps
    weights = mix[1] * temps
    student_inverse = jnp.concatenate([jnp.full((1,), LOG2E, jnp.float32), inverse])
    scalars = jnp.stack([student_inverse, jnp.concatenate([mix[:1], weights])])
    relative = jnp.arange(0, count_vocab, 2, dtype=jnp.int32)
    keep_order = me_vocab ^ relative
    send_order = me_vocab ^ (relative + 1)

    def partial_logits(gathered):
        partial = jnp.dot(gathered, head, preferred_element_type=jnp.float32)
        return partial.reshape(*[2] * len(dp_masks), part, width)

    def reduced(partial, masks):
        left = dp_masks
        for mask in masks:
            axis, bit = left.index(mask), (me_dp // mask) % 2
            other = swap(pick(partial, 1 - bit, axis).astype(jnp.float16), "dp", mask)
            partial = pick(partial, bit, axis) + other.astype(jnp.float32)
            left = [m for m in left if m != mask]
        return partial

    def merged(student, fixed):
        stats = jnp.concatenate([student, fixed])
        for mask in near:
            other = swap(stats, "vocab", mask)
            stats = jnp.concatenate(
                [
                    merge(stats[:8], other[:8], student_inverse[:, None]),
                    merge(stats[8:], other[8:], inverse[:, None]),
                ]
            )
        return stats

    def products(blocks, grad):
        return lax.dot_general(blocks, grad, (((2,), (1,)), ((), ())), preferred_element_type=jnp.float32)

    def folded(sides, masks):
        sent = [[k for k in sorted(side) if k & mask] for side, mask in zip(sides, masks)]
        others = [
            swap(jnp.stack([side[k].astype(jnp.bfloat16) for k in keys]), "vocab", mask)
            for side, keys, mask in zip(sides, sent, masks)
        ]
        others = lax.optimization_barrier(others)
        return [
            {k ^ mask: side[k ^ mask] + other[n].astype(jnp.float32) for n, k in enumerate(keys)}
            for side, keys, mask, other in zip(sides, sent, masks, others)
        ]

    def split(blocks):
        return [{k: blocks[k][: rows // 2] for k in blocks}, {k: blocks[k][rows // 2 :] for k in blocks}]

    have, cross = [], []
    for c in range(CHUNKS):
        block = own[c * count_dp * part : (c + 1) * count_dp * part][None]
        have.append({0: block})
        cross.append({1: swap(block, "vocab", 1)})
    own_stats = local_stats([teacher], CHUNKS, inverse)
    for step in range(len(far) - 1):
        arrived = []
        for c in range(CHUNKS):
            mask = far[:-1][step] if c % 2 else near[1:][step]
            keys = sorted(have[c])
            arrived.append((keys, mask, swap(jnp.concatenate([have[c][k] for k in keys]), "vocab", mask)))
        for c, (keys, mask, other) in enumerate(arrived):
            other_cross = swap(other, "vocab", 1)
            for place, k in enumerate(keys):
                have[c][k ^ mask] = other[place : place + 1]
                cross[c][k ^ mask ^ 1] = other_cross[place : place + 1]
        if step == 0:
            own_stats, have = lax.optimization_barrier((own_stats, have))

    gathered, partials = [], []
    for c in range(CHUNKS):
        found = have[c] | cross[c]
        found = jnp.concatenate([found[k] for k in range(count_vocab)])
        gathered.append(jnp.concatenate([pick(found, me_vocab ^ n) for n in range(count_vocab)], axis=1))
        partials.append(partial_logits(gathered[c]))
    logits = [
        reduced(partials[c], dp_masks if c % 2 else dp_masks[::-1]) for c in range(CHUNKS)
    ]
    place = (labels - me_vocab * width).astype(jnp.float32).reshape(CHUNKS, part)
    place = jnp.pad(place, ((0, 0), (0, padded(part) - part))).reshape(1, -1)
    stats = merged(local_stats(logits, 1, student_inverse), own_stats)
    stats = jnp.split(jnp.concatenate([stats[:15], place]), CHUNKS, axis=1)

    cuts = [0, FIRST, tokens]
    grads, arrived = [], []
    for first, last in zip(cuts, cuts[1:]):
        if grads:
            grads[-1], logits = lax.optimization_barrier((grads[-1], logits))
        grads.append(logit_grad(first, last, logits, teacher, stats, scalars))

    def crossing(c):
        arrived[c] = lax.optimization_barrier(arrived[c])
        found = jnp.stack([grads[c]] + [arrived[c][r] for r in range(1, count_dp)])
        grad_all = jnp.concatenate([pick(found, me_dp ^ n) for n in range(count_dp)])
        grad_all = lax.optimization_barrier(grad_all)
        crossed = swap(products(head_send, grad_all).astype(jnp.bfloat16), "vocab", 1)
        return crossed, grad_all

    def kept(crossed, grad_all):
        keep = products(head_keep, grad_all)
        return {2 * k: keep[k] + crossed[k].astype(jnp.float32) for k in range(count_vocab // 2)}

    arrived = [None, None]
    def exchange(grad):
        return {r: swap(grad, "dp", r) for r in range(1, count_dp)}

    arrived[0] = exchange(grads[0])
    grads[1], head = lax.optimization_barrier((grads[1], head))
    head_send, head_keep = row_blocks(head, jnp.stack([send_order, keep_order]), rows)
    grads[1], head_send, head_keep, arrived[0] = lax.optimization_barrier((grads[1], head_send, head_keep, arrived[0]))
    arrived[1] = exchange(grads[1])
    steps = list(zip(near[1:], far))
    all_grads = [None, None]
    crossed, all_grads[0] = crossing(0)
    early = kept(crossed, all_grads[0])
    early, arrived[1][1] = lax.optimization_barrier((early, arrived[1][1]))
    early = split(early)
    early = folded(early, steps[0])
    crossed, all_grads[1] = crossing(1)
    late = kept(crossed, all_grads[1])
    early, late, all_grads = lax.optimization_barrier((early, late, all_grads))
    for step in steps[1:]:
        early = folded(early, step)
    head_grad = lax.dot_general(
        jnp.concatenate(gathered, axis=0),
        jnp.concatenate([g.reshape(count_dp, -1, width) for g in all_grads], axis=1)
        .reshape(count_dp, CHUNKS, part, width)
        .transpose(1, 0, 2, 3)
        .reshape(-1, width),
        (((0,), (0,)), ((), ())),
        preferred_element_type=jnp.float32,
    ).astype(jnp.bfloat16)
    late = split(late)
    for step in steps:
        late = folded(late, step)
    hidden_parts = [jnp.concatenate([side[0] for side in sides]) for sides in (early, late)]
    hidden_grad = jnp.concatenate([p.reshape(rows, count_dp, -1) for p in hidden_parts], axis=2)
    return (hidden_grad.reshape(rows, count_dp * tokens), head_grad)


def solution(mesh):
    placed = (P(("dp", "vocab"), None), P("dp", "vocab"), P("dp", "vocab"), P("dp"), P(), P())
    return jax.shard_map(
        shards,
        mesh=mesh,
        in_specs=placed,
        out_specs=(P(("dp", "vocab"), None), P("dp", "vocab")),
        check_vma=False,
    )
```

```python
import functools

import jax
import jax.numpy as jnp
from jax import lax
from jax.experimental import pallas as pl
from jax.experimental.pallas import tpu as pltpu
from jax.sharding import PartitionSpec as P

CHUNKS = 2
FIRST = 96
STRIP = 96
LANES = 128
LOG2E = 1.4426950408889634


def swap(value, axis, mask):
    count = lax.axis_size(axis)
    return lax.ppermute(value, axis, [(k, k ^ mask) for k in range(count)])


def masks_far_first(count):
    mask = count // 2
    while mask:
        yield mask
        mask //= 2


def pick(parts, place, axis=0):
    return lax.dynamic_index_in_dim(parts, place, axis, keepdims=False)


def padded(count):
    return -(-count // LANES) * LANES


VMEM = pl.BlockSpec(memory_space=pltpu.VMEM)
SMEM = pl.BlockSpec(memory_space=pltpu.SMEM)


def stats_kernel(heats, pieces, inverse_ref, *refs):
    *values, out_ref, column = refs
    column[...] = jnp.zeros_like(column)
    lane = lax.broadcasted_iota(jnp.int32, (STRIP, LANES), 1)
    chunks = len(values) * pieces
    part = values[0].shape[0] // pieces
    for chunk in range(chunks):
        x_ref, start = values[chunk // pieces], chunk % pieces * part
        base = chunk * padded(part)

        @pl.loop(0, part // STRIP)
        def _(strip):
            row = pl.multiple_of(strip * STRIP, STRIP)
            x = x_ref[pl.ds(start + row, STRIP), :].astype(jnp.float32)
            peak = jnp.max(x, axis=1, keepdims=True)
            x = x - peak
            record = jnp.where(lane == 0, peak, 0.0)
            for k in range(heats):
                total = jnp.sum(jnp.exp2(x * inverse_ref[k]), axis=1, keepdims=True)
                record = jnp.where(lane == k + 1, total, record)
            column[pl.ds(base + row, STRIP), :] = record

    out_ref[...] = column[...].T[: out_ref.shape[0], :]


def local_stats(values, pieces, inverse):
    tokens, heats = values[0].shape[0] // pieces, inverse.shape[0]
    lanes = len(values) * pieces * padded(tokens)
    size = len(values) * values[0].size
    return pl.pallas_call(
        functools.partial(stats_kernel, heats, pieces),
        out_shape=jax.ShapeDtypeStruct((8, lanes), jnp.float32),
        in_specs=[SMEM] + [VMEM] * len(values),
        out_specs=VMEM,
        scratch_shapes=[pltpu.VMEM((lanes, LANES), jnp.float32)],
        compiler_params=pltpu.CompilerParams(vmem_limit_bytes=4 << 20),
        cost_estimate=pl.CostEstimate(flops=2 * heats * size, bytes_accessed=2 * size, transcendentals=heats * size),
        name="stats",
    )(inverse, *values)


def grad_kernel(heats, pieces, scalars_ref, teacher_ref, *refs):
    values, stats, (out_ref, column) = refs[: len(pieces)], refs[len(pieces) : -2], refs[-2:]
    width = teacher_ref.shape[1]
    lane = lax.broadcasted_iota(jnp.int32, (STRIP, width), 1).astype(jnp.float32)
    done = 0
    for x_ref, stats_ref, (start, token, count) in zip(values, stats, pieces):
        column[...] = stats_ref[...].T
        base = done

        @pl.loop(0, count // STRIP)
        def _(strip):
            row = pl.multiple_of(strip * STRIP, STRIP)
            record = column[pl.ds(start + row, STRIP), :]
            x = x_ref[pl.ds(start + row, STRIP), :] - record[:, 0:1]
            t = teacher_ref[pl.ds(token + row, STRIP), :].astype(jnp.float32) - record[:, 8:9]
            result = jnp.exp2(x * scalars_ref[0, 0]) * (scalars_ref[1, 0] / record[:, 1:2])
            result = result - jnp.where(lane == record[:, 15:16], scalars_ref[1, 0], 0.0)
            for k in range(1, heats + 1):
                scale, factor = scalars_ref[0, k], scalars_ref[1, k]
                result = result + jnp.exp2(x * scale) * (factor / record[:, k + 1 : k + 2])
                result = result - jnp.exp2(t * scale) * (factor / record[:, k + 8 : k + 9])
            out_ref[pl.ds(base + row, STRIP), :] = result.astype(out_ref.dtype)

        done += count


def logit_grad(first, last, logits, teacher, stats, scalars):
    heats = scalars.shape[1] - 1
    part, width = logits[0].shape
    pieces, values, records = [], [], []
    for c in range(len(logits)):
        low, high = max(first, c * part), min(last, (c + 1) * part)
        if low < high:
            pieces.append((low - c * part, low, high - low))
            values.append(logits[c])
            records.append(stats[c])
    size = (last - first) * width
    return pl.pallas_call(
        functools.partial(grad_kernel, heats, pieces),
        out_shape=jax.ShapeDtypeStruct((last - first, width), jnp.bfloat16),
        in_specs=[SMEM] + [VMEM] * (1 + 2 * len(pieces)),
        out_specs=VMEM,
        scratch_shapes=[pltpu.VMEM((padded(part), stats[0].shape[0]), jnp.float32)],
        compiler_params=pltpu.CompilerParams(vmem_limit_bytes=4 << 20),
        cost_estimate=pl.CostEstimate(
            flops=6 * heats * size, bytes_accessed=8 * size, transcendentals=2 * heats * size
        ),
        name="grad",
    )(scalars, teacher, *values, *records)


def merge(mine, other, inverse):
    heats = inverse.shape[0]
    highest = jnp.maximum(mine[0:1], other[0:1])
    total = mine[1 : heats + 1] * jnp.exp2((mine[0:1] - highest) * inverse) + other[1 : heats + 1] * jnp.exp2(
        (other[0:1] - highest) * inverse
    )
    return jnp.concatenate([highest, total, mine[heats + 1 :]], axis=0)


def copy_kernel(rows, order_ref, in_ref, *refs):
    *out_refs, held, come, gone = refs
    inward, outward = [], []
    for side, out_ref in enumerate(out_refs):
        for k in range(out_ref.shape[0]):
            start = pl.multiple_of(order_ref[side, k] * rows, rows)
            slot = side * out_ref.shape[0] + k
            inward.append(pltpu.make_async_copy(in_ref.at[pl.ds(start, rows)], held.at[slot], come.at[slot]))
            outward.append(pltpu.make_async_copy(held.at[slot], out_ref.at[k], gone.at[slot]))
    for copy in inward:
        copy.start()
    for come_copy, gone_copy in zip(inward, outward):
        come_copy.wait()
        gone_copy.start()
    for copy in outward:
        copy.wait()


def row_blocks(array, order, rows):
    sides, count = order.shape
    block = jax.ShapeDtypeStruct((count, rows, array.shape[1]), array.dtype)
    hbm = pl.BlockSpec(memory_space=pltpu.HBM)
    return pl.pallas_call(
        functools.partial(copy_kernel, rows),
        out_shape=[block] * sides,
        in_specs=[SMEM, hbm],
        out_specs=[hbm] * sides,
        scratch_shapes=[
            pltpu.VMEM((sides * count, rows, array.shape[1]), array.dtype),
            pltpu.SemaphoreType.DMA((sides * count,)),
            pltpu.SemaphoreType.DMA((sides * count,)),
        ],
        compiler_params=pltpu.CompilerParams(vmem_limit_bytes=8 << 20),
        cost_estimate=pl.CostEstimate(flops=0, bytes_accessed=4 * array.size, transcendentals=0),
        name="row_blocks",
    )(order, array)


def shards(hidden_t, head, teacher, labels, temps, mix):
    count_dp, count_vocab = lax.axis_size("dp"), lax.axis_size("vocab")
    me_dp, me_vocab = lax.axis_index("dp"), lax.axis_index("vocab")
    rows = hidden_t.shape[0]
    tokens, width = teacher.shape
    part = tokens // CHUNKS
    heats = temps.shape[0]
    far = list(masks_far_first(count_vocab))
    near = far[::-1]
    dp_masks = list(masks_far_first(count_dp))

    own = hidden_t.T.reshape(count_dp, CHUNKS, part, rows).transpose(1, 0, 2, 3).reshape(-1, rows)

    inverse = LOG2E / temps
    weights = mix[1] * temps
    student_inverse = jnp.concatenate([jnp.full((1,), LOG2E, jnp.float32), inverse])
    scalars = jnp.stack([student_inverse, jnp.concatenate([mix[:1], weights])])
    relative = jnp.arange(0, count_vocab, 2, dtype=jnp.int32)
    keep_order = me_vocab ^ relative
    send_order = me_vocab ^ (relative + 1)

    def partial_logits(gathered):
        partial = jnp.dot(gathered, head, preferred_element_type=jnp.float32)
        return partial.reshape(*[2] * len(dp_masks), part, width)

    def reduced(partial, masks):
        left = dp_masks
        for mask in masks:
            axis, bit = left.index(mask), (me_dp // mask) % 2
            other = swap(pick(partial, 1 - bit, axis).astype(jnp.float16), "dp", mask)
            partial = pick(partial, bit, axis) + other.astype(jnp.float32)
            left = [m for m in left if m != mask]
        return partial

    def merged(student, fixed):
        stats = jnp.concatenate([student, fixed])
        for mask in near:
            other = swap(stats, "vocab", mask)
            stats = jnp.concatenate(
                [
                    merge(stats[:8], other[:8], student_inverse[:, None]),
                    merge(stats[8:], other[8:], inverse[:, None]),
                ]
            )
        return stats

    def products(blocks, grad):
        return lax.dot_general(blocks, grad, (((2,), (1,)), ((), ())), preferred_element_type=jnp.float32)

    def folded(sides, masks):
        sent = [[k for k in sorted(side) if k & mask] for side, mask in zip(sides, masks)]
        others = [
            swap(jnp.stack([side[k].astype(jnp.bfloat16) for k in keys]), "vocab", mask)
            for side, keys, mask in zip(sides, sent, masks)
        ]
        others = lax.optimization_barrier(others)
        return [
            {k ^ mask: side[k ^ mask] + other[n].astype(jnp.float32) for n, k in enumerate(keys)}
            for side, keys, mask, other in zip(sides, sent, masks, others)
        ]

    def split(blocks):
        return [{k: blocks[k][: rows // 2] for k in blocks}, {k: blocks[k][rows // 2 :] for k in blocks}]

    have, cross = [], []
    for c in range(CHUNKS):
        block = own[c * count_dp * part : (c + 1) * count_dp * part][None]
        have.append({0: block})
        cross.append({1: swap(block, "vocab", 1)})
    own_stats = local_stats([teacher], CHUNKS, inverse)
    for step in range(len(far) - 1):
        arrived = []
        for c in range(CHUNKS):
            mask = far[:-1][step] if c % 2 else near[1:][step]
            keys = sorted(have[c])
            arrived.append((keys, mask, swap(jnp.concatenate([have[c][k] for k in keys]), "vocab", mask)))
        for c, (keys, mask, other) in enumerate(arrived):
            other_cross = swap(other, "vocab", 1)
            for place, k in enumerate(keys):
                have[c][k ^ mask] = other[place : place + 1]
                cross[c][k ^ mask ^ 1] = other_cross[place : place + 1]
        if step == 0:
            own_stats, have = lax.optimization_barrier((own_stats, have))

    gathered, partials = [], []
    for c in range(CHUNKS):
        found = have[c] | cross[c]
        found = jnp.concatenate([found[k] for k in range(count_vocab)])
        gathered.append(jnp.concatenate([pick(found, me_vocab ^ n) for n in range(count_vocab)], axis=1))
        partials.append(partial_logits(gathered[c]))
    logits = [
        reduced(partials[c], dp_masks if c % 2 else dp_masks[::-1]) for c in range(CHUNKS)
    ]
    place = (labels - me_vocab * width).astype(jnp.float32).reshape(CHUNKS, part)
    place = jnp.pad(place, ((0, 0), (0, padded(part) - part))).reshape(1, -1)
    stats = merged(local_stats(logits, 1, student_inverse), own_stats)
    stats = jnp.split(jnp.concatenate([stats[:15], place]), CHUNKS, axis=1)

    cuts = [0, FIRST, tokens]
    grads, arrived = [], []
    for first, last in zip(cuts, cuts[1:]):
        if grads:
            grads[-1], logits = lax.optimization_barrier((grads[-1], logits))
        grads.append(logit_grad(first, last, logits, teacher, stats, scalars))

    def crossing(c):
        arrived[c] = lax.optimization_barrier(arrived[c])
        found = jnp.stack([grads[c]] + [arrived[c][r] for r in range(1, count_dp)])
        grad_all = jnp.concatenate([pick(found, me_dp ^ n) for n in range(count_dp)])
        grad_all = lax.optimization_barrier(grad_all)
        crossed = swap(products(head_send, grad_all).astype(jnp.bfloat16), "vocab", 1)
        return crossed, grad_all

    def kept(crossed, grad_all):
        keep = products(head_keep, grad_all)
        return {2 * k: keep[k] + crossed[k].astype(jnp.float32) for k in range(count_vocab // 2)}

    arrived = [None, None]
    def exchange(grad):
        return {r: swap(grad, "dp", r) for r in reversed(range(1, count_dp))}

    arrived[0] = exchange(grads[0])
    grads[1], head = lax.optimization_barrier((grads[1], head))
    head_send, head_keep = row_blocks(head, jnp.stack([send_order, keep_order]), rows)
    grads[1], head_send, head_keep, arrived[0] = lax.optimization_barrier((grads[1], head_send, head_keep, arrived[0]))
    arrived[1] = exchange(grads[1])
    steps = list(zip(near[1:], far))
    all_grads = [None, None]
    crossed, all_grads[0] = crossing(0)
    early = kept(crossed, all_grads[0])
    early, arrived[1][1] = lax.optimization_barrier((early, arrived[1][1]))
    early = split(early)
    early = folded(early, steps[0])
    crossed, all_grads[1] = crossing(1)
    late = kept(crossed, all_grads[1])
    early, late, all_grads = lax.optimization_barrier((early, late, all_grads))
    for step in steps[1:]:
        early = folded(early, step)
    head_grad = lax.dot_general(
        jnp.concatenate(gathered, axis=0),
        jnp.concatenate([g.reshape(count_dp, -1, width) for g in all_grads], axis=1)
        .reshape(count_dp, CHUNKS, part, width)
        .transpose(1, 0, 2, 3)
        .reshape(-1, width),
        (((0,), (0,)), ((), ())),
        preferred_element_type=jnp.float32,
    ).astype(jnp.bfloat16)
    late = split(late)
    for step in steps:
        late = folded(late, step)
    hidden_parts = [jnp.concatenate([side[0] for side in sides]) for sides in (early, late)]
    hidden_grad = jnp.concatenate([p.reshape(rows, count_dp, -1) for p in hidden_parts], axis=2)
    return (hidden_grad.reshape(rows, count_dp * tokens), head_grad)


def solution(mesh):
    placed = (P(("dp", "vocab"), None), P("dp", "vocab"), P("dp", "vocab"), P("dp"), P(), P())
    return jax.shard_map(
        shards,
        mesh=mesh,
        in_specs=placed,
        out_specs=(P(("dp", "vocab"), None), P("dp", "vocab")),
        check_vma=False,
    )
```
